32 devices in a mesh: dp: 8 (over z, core), ctx: 4 (over y, x).
Axes of the slice: x: 2, y: 2, z: 4, core: 2. Of those that a mesh axis runs over, the one named last changes fastest.
Arguments:
- actions: bfloat16 [8, 512, 1024], P('dp', 'ctx'), may hold values from -6 to 6
- stamps: int32 [8, 512], P('dp', 'ctx'), may hold values from 0 to 65408, as said below
- lengths: int32 [8], P('dp'), may hold values from 128 to 512, as said below
- w_proj: bfloat16 [1024, 1024], replicated, may hold values from -0.1875 to 0.1875
- w_out: bfloat16 [256, 1024], replicated, may hold values from -0.375 to 0.375
- bias_table: float32 [16, 4], replicated, may hold values from -4 to 4
- grad_out: bfloat16 [8, 512, 1024], P('dp', 'ctx'), may hold values from -6 to 6
Outputs:
- layer_out: bfloat16 [8, 512, 1024], P('dp', 'ctx')
- grad_actions: bfloat16 [8, 512, 1024], P('dp', 'ctx')
- grad_table: float32 [16, 4], replicated
The draws below stay inside these ranges and needn't reach their ends.
Inputs may be any that keep to these rules, and one draw needn't show every extreme that they name: lengths 512 and 128 occur in every draw. `stamps`: non-decreasing along each row from 0, by steps of 1 to 128.
All inputs are finite; a program needn't handle non-finite values.
Results may differ from the reference program's by a relative error of at most 0.0077.
Values may be sent and summed in bfloat16 or wider, within the bound.
A program may use at most 64 MiB of HBM per device.

```python
import jax
import jax.numpy as jnp
from jax import lax

D = 1024
HEADS = 4
HEAD = 64
NBKT = 16
ATT = 256
SEQ_LEN = 512
USERS = 8
ALL_TOKENS = 4096


def draw_stamps(key, part):
    key = jax.random.fold_in(key, 11)
    powers = jax.random.randint(key, (USERS, SEQ_LEN), 0, 8)
    powers = powers.at[0].set(7)
    step_gaps = jnp.left_shift(jnp.ones_like(powers), powers)
    totals = jnp.cumsum(step_gaps, axis=1)
    return (totals - step_gaps[:, :1]).astype(jnp.int32)


def draw_lengths(key, part):
    key = jax.random.fold_in(key, 23)
    drawn = jax.random.randint(key, (USERS,), SEQ_LEN // 4, SEQ_LEN + 1)
    return drawn.at[0].set(SEQ_LEN).at[1].set(SEQ_LEN // 4).astype(jnp.int32)


def levels(key, shape, split, smallest, high):
    gain, own = 1.0, jax.random.fold_in(key, 6)
    for position, blocks in split:
        steps = jnp.exp(jax.random.uniform(jax.random.fold_in(own, position), (blocks,), jnp.float32, smallest / len(split), high / len(split)))
        gain = gain * jnp.repeat(steps, shape[position] // blocks).reshape([-1 if axis == position else 1 for axis in range(len(shape))])
    return gain


def normal_values(rng, shape, width, most, pieces=(), held_as=jnp.bfloat16):
    values = jax.random.normal(rng, shape, jnp.float32) * width
    if len(pieces) > 0:
        values = levels(rng, shape, pieces, -0.22, 0.18) * values
    return jnp.clip(values, min=-most, max=most).astype(held_as)


def setup_inputs(seed: int = 0) -> dict:
    key_of = jax.random.split(jax.random.key(seed), 8)
    actions = normal_values(key_of[0], (USERS, SEQ_LEN, D), 1.0, 6.0, ((0, 8), (1, 4)))
    stamps = draw_stamps(jax.random.fold_in(key_of[7], 71), 0)
    lengths = draw_lengths(jax.random.fold_in(key_of[7], 71), 0)
    w_proj = normal_values(key_of[3], (D, 4 * ATT), D ** -0.5, 0.1875)
    w_out = normal_values(key_of[4], (ATT, D), ATT ** -0.5, 0.375)
    bias_table = normal_values(key_of[5], (NBKT, HEADS), 1.0, 4.0, (), jnp.float32)
    grad_out = normal_values(key_of[6], (USERS, SEQ_LEN, D), 1.0, 6.0, ((0, 8), (1, 4)))
    return dict(actions=actions, stamps=stamps, lengths=lengths, w_proj=w_proj, w_out=w_out, bias_table=bias_table, grad_out=grad_out)


EPS = 1e-05

def norm_rows(values):
    row_mean = lax.optimization_barrier(jnp.mean(values, axis=-1, keepdims=True))
    centred = values - row_mean
    spread = lax.optimization_barrier(jnp.mean(centred * centred, axis=-1, keepdims=True))
    inverse = lax.rsqrt(spread + EPS)
    return (centred * inverse, inverse)

def norm_back(incoming, normed, inverse):
    first = lax.optimization_barrier(jnp.mean(incoming, axis=-1, keepdims=True))
    second = lax.optimization_barrier(jnp.mean(incoming * normed, axis=-1, keepdims=True))
    return inverse * (incoming - first - normed * second)

def silu_slope(values):
    sigmoid_val = jax.nn.sigmoid(values)
    return sigmoid_val * (1.0 + values * (1.0 - sigmoid_val))

def bucket_bias(query_stamps, key_stamps, table_vals):
    stamp_gap = query_stamps[:, None] - key_stamps[None, :]
    bias_sum = jnp.zeros((table_vals.shape[1],) + stamp_gap.shape, jnp.float32) + table_vals[0][:, None, None]
    for level_index in range(table_vals.shape[0] - 1):
        above_level = (stamp_gap >= 1 << level_index).astype(jnp.float32)
        bias_sum = bias_sum + above_level[None] * (table_vals[level_index + 1] - table_vals[level_index])[:, None, None]
    return bias_sum

def bucket_index(query_stamps, key_stamps, level_count):
    stamp_gap = query_stamps[:, None] - key_stamps[None, :]
    found = jnp.zeros(stamp_gap.shape, jnp.int32)
    for level_index in range(level_count - 1):
        found = found + (stamp_gap >= 1 << level_index).astype(jnp.int32)
    return found

def table_terms(grad_scores, buckets, level_count):
    rows = [lax.optimization_barrier(jnp.sum(jnp.where(buckets[None] == level_index, grad_scores, 0.0), axis=(1, 2))) for level_index in range(level_count)]
    return jnp.stack(rows, axis=0)

def reference(actions, stamps, lengths, w_proj, w_out, bias_table, grad_out):
    score_scale = HEAD ** (-0.5)
    block_rows = min(512, SEQ_LEN)
    block_count = SEQ_LEN // block_rows
    positions = jnp.arange(SEQ_LEN).astype(jnp.int32)

    def one_user(table_acc, items):
        inputs, own_stamps, upstream, length = items
        normed, inverse = norm_rows(inputs.astype(jnp.float32))
        pre_act = jnp.dot(normed.astype(jnp.bfloat16), w_proj, preferred_element_type=jnp.float32)
        activated = jax.nn.silu(pre_act).astype(jnp.bfloat16)
        gate_units = activated[:, :ATT].astype(jnp.float32)
        queries = activated[:, ATT:2 * ATT]
        key_heads = activated[:, 2 * ATT:3 * ATT].astype(jnp.float32).reshape(SEQ_LEN, HEADS, HEAD)
        value_heads = activated[:, 3 * ATT:].astype(jnp.float32).reshape(SEQ_LEN, HEADS, HEAD)
        counts = (jnp.minimum(positions, length - 1) + 1).astype(jnp.float32)

        def one_block(carry, block_index):
            grad_k_acc, grad_v_acc, table_sum = carry
            start = (block_index * block_rows).astype(jnp.int32)
            query_rows = lax.dynamic_slice_in_dim(queries, start, block_rows, 0)
            gate_rows = lax.dynamic_slice_in_dim(gate_units, start, block_rows, 0)
            input_rows = lax.dynamic_slice_in_dim(inputs, start, block_rows, 0)
            up_rows = lax.dynamic_slice_in_dim(upstream, start, block_rows, 0)
            stamp_rows = lax.dynamic_slice_in_dim(own_stamps, start, block_rows, 0)
            count_rows = lax.dynamic_slice_in_dim(counts, start, block_rows, 0)
            query_pos = lax.dynamic_slice_in_dim(positions, start, block_rows, 0)
            query_heads = query_rows.astype(jnp.float32).reshape(block_rows, HEADS, HEAD)
            visible = (positions[None, :] <= query_pos[:, None]) & (positions[None, :] < length)
            scores = jnp.einsum('qhd,khd->hqk', query_heads, key_heads) * score_scale + bucket_bias(stamp_rows, own_stamps, bias_table)
            weights = (jnp.where(visible[None], jax.nn.silu(scores), 0.0) / count_rows[None, :, None]).astype(jnp.bfloat16)
            mixed_out = jnp.einsum('hqk,khd->qhd', weights.astype(jnp.float32), value_heads).reshape(block_rows, ATT)
            mixed_norm, mixed_inv = norm_rows(mixed_out)
            gated_rows = (mixed_norm * gate_rows).astype(jnp.bfloat16)
            layer_rows = (input_rows.astype(jnp.float32) + jnp.dot(gated_rows, w_out, preferred_element_type=jnp.float32)).astype(jnp.bfloat16)
            grad_gated = jnp.dot(up_rows, w_out.T, preferred_element_type=jnp.float32)
            grad_units = grad_gated * mixed_norm
            grad_mixed = norm_back(grad_gated * gate_rows, mixed_norm, mixed_inv).astype(jnp.bfloat16)
            grad_heads = grad_mixed.astype(jnp.float32).reshape(block_rows, HEADS, HEAD)
            grad_weights = jnp.einsum('qhd,khd->hqk', grad_heads, value_heads)
            grad_v_acc = grad_v_acc + jnp.einsum('hqk,qhd->khd', weights.astype(jnp.float32), grad_heads)
            grad_scores = (jnp.where(visible[None], grad_weights * silu_slope(scores), 0.0) / count_rows[None, :, None]).astype(jnp.bfloat16)
            scores_f = grad_scores.astype(jnp.float32)
            grad_queries = jnp.einsum('hqk,khd->qhd', scores_f, key_heads) * score_scale
            grad_k_acc = grad_k_acc + jnp.einsum('hqk,qhd->khd', scores_f, query_heads) * score_scale
            table_sum = table_sum + table_terms(scores_f, bucket_index(stamp_rows, own_stamps, NBKT), NBKT)
            return ((grad_k_acc, grad_v_acc, table_sum), (layer_rows, grad_units, grad_queries.reshape(block_rows, ATT)))
        start_carry = (jnp.zeros((SEQ_LEN, HEADS, HEAD), jnp.float32), jnp.zeros((SEQ_LEN, HEADS, HEAD), jnp.float32), table_acc)
        (grad_keys, grad_values, table_acc), (layer_blocks, unit_blocks, query_blocks) = lax.scan(one_block, start_carry, jnp.arange(block_count).astype(jnp.int32))
        layer_rows = layer_blocks.reshape(SEQ_LEN, D)
        grad_act = jnp.concatenate([unit_blocks.reshape(SEQ_LEN, ATT), query_blocks.reshape(SEQ_LEN, ATT), grad_keys.reshape(SEQ_LEN, ATT), grad_values.reshape(SEQ_LEN, ATT)], axis=1)
        grad_pre = (grad_act * silu_slope(pre_act)).astype(jnp.bfloat16)
        grad_normed = jnp.dot(grad_pre, w_proj.T, preferred_element_type=jnp.float32)
        grad_rows = (norm_back(grad_normed, normed, inverse) + upstream.astype(jnp.float32)).astype(jnp.bfloat16)
        return (table_acc, (layer_rows, grad_rows))
    start_table = jnp.zeros((NBKT, HEADS), jnp.float32)
    table_total, (layer_all, grad_all) = lax.scan(one_user, start_table, (actions, stamps, grad_out, lengths))
    grad_table = table_total * (1.0 / ALL_TOKENS ** 0.5)
    return (layer_all, grad_all, grad_table)
```

```python
import functools
import math

import jax
import jax.numpy as jnp
from jax import lax
from jax.experimental import pallas as pl
from jax.experimental.pallas import tpu as pltpu
from jax.sharding import PartitionSpec as P

EPS = 1e-05
MESH = pl.DeviceIdType.MESH
LANES = 128
F32 = jnp.float32
BF16 = jnp.bfloat16
NT = (((1,), (1,)), ((), ()))
TN = (((0,), (0,)), ((), ()))
NN = (((1,), (0,)), ((), ()))


def mul(left, right, dims=NN):
    return lax.dot_general(left, right, dims, preferred_element_type=F32)


def sigmoid(values):
    return 0.5 * jnp.tanh(0.5 * values) + 0.5


def norm_rows(values):
    row_mean = jnp.mean(values, axis=-1, keepdims=True)
    centred = values - row_mean
    spread = jnp.mean(centred * centred, axis=-1, keepdims=True)
    inverse = lax.rsqrt(spread + EPS)
    return centred * inverse, inverse


def norm_back(incoming, normed, inverse):
    first = jnp.mean(incoming, axis=-1, keepdims=True)
    second = jnp.mean(incoming * normed, axis=-1, keepdims=True)
    return inverse * (incoming - first - normed * second)


def silu_slope(values):
    sig = sigmoid(values)
    return sig * (1.0 + values * (1.0 - sig))


def kernel(
    ctx_count, data_count, head_count, level_count, scale_table,
    len_ref, table_ref, stamps_ref, x_hbm, wp_hbm, wo_hbm, go_hbm,
    layer_hbm, grad_hbm, gt_ref,
    xv, wp, wo, go, normed_ref, pre_ref, gate_ref, kv_all, st_all, scol, steps,
    qs, gs, buckets, sc, wt, mix, dq, own, snd, rcv, tab1, tab2, tacc,
    layer_v, grad_v,
    load_sem, out_sem, st_send, st_recv, kv_send, kv_recv, d_send, d_recv,
    t1_send, t1_recv, t2_send, t2_recv,
):
    rows, model_dim = xv.shape
    att = wo.shape[0]
    head_dim = att // head_count
    per = LANES // head_dim
    groups = att // LANES
    score_scale = head_dim ** (-0.5)
    me = lax.axis_index("ctx")
    my_dp = lax.axis_index("dp")
    ctx_at = lambda rank: {"ctx": rank}
    dp_at = lambda rank: {"dp": rank}

    def remote(src, dst, send_sem, recv_sem, where):
        return pltpu.make_async_remote_copy(
            src_ref=src, dst_ref=dst, send_sem=send_sem, recv_sem=recv_sem,
            device_id=where, device_id_type=MESH,
        )

    def loop(low, high, body):
        def step(index, carry):
            body(index)
            return carry

        lax.fori_loop(low, high, step, 0)

    load_x = pltpu.make_async_copy(x_hbm, xv, load_sem.at[0])
    load_kv = pltpu.make_async_copy(
        wp_hbm.at[:, pl.ds(2 * att, 2 * att)], wp.at[:, pl.ds(2 * att, 2 * att)], load_sem.at[1]
    )
    load_uq = pltpu.make_async_copy(
        wp_hbm.at[:, pl.ds(0, 2 * att)], wp.at[:, pl.ds(0, 2 * att)], load_sem.at[2]
    )
    load_go = pltpu.make_async_copy(go_hbm, go, load_sem.at[3])
    load_wo = pltpu.make_async_copy(wo_hbm, wo, load_sem.at[4])
    for load in (load_x, load_kv, load_uq, load_go, load_wo):
        load.start()

    barrier = pltpu.get_barrier_semaphore()
    ctx_peer = lambda offset: lax.rem(me + offset, ctx_count)
    dp_peer = lambda offset: lax.rem(my_dp + offset, data_count)

    @functools.partial(loop, 1, ctx_count)
    def _(offset):
        pl.semaphore_signal(
            barrier, inc=1, device_id=ctx_at(ctx_peer(offset)), device_id_type=MESH
        )

    @functools.partial(loop, 1, data_count)
    def _(offset):
        pl.semaphore_signal(
            barrier, inc=1, device_id=dp_at(dp_peer(offset)), device_id_type=MESH
        )

    length = len_ref[0]
    for head in range(head_count):
        running = table_ref[0, head]
        steps[0, head] = running
        for level in range(level_count - 1):
            running = running + (table_ref[level + 1, head] - table_ref[level, head])
            steps[level + 1, head] = running

    stamp_row = stamps_ref[...]
    st_all[me] = jnp.broadcast_to(stamp_row, (8, LANES))
    scol[...] = jnp.broadcast_to(stamp_row, (rows, LANES)).T

    load_x.wait()
    normed, inverse = norm_rows(xv[...].astype(F32))
    normed_ref[...] = normed
    rounded = normed.astype(BF16)
    load_kv.wait()
    pre_kv = mul(rounded, wp[:, 2 * att :])
    pre_ref[:, 2 * att :] = pre_kv
    kv_all[me] = (pre_kv * sigmoid(pre_kv)).astype(BF16)

    pl.semaphore_wait(barrier, ctx_count - 1 + data_count - 1)

    @functools.partial(loop, me + 1, ctx_count)
    def _(rank):
        remote(
            st_all.at[me], st_all.at[me], st_send.at[rank], st_recv.at[me], ctx_at(rank)
        ).start()

    @functools.partial(loop, me + 1, ctx_count)
    def _(rank):
        remote(
            kv_all.at[me], kv_all.at[me], kv_send.at[rank], kv_recv.at[me], ctx_at(rank)
        ).start()

    lane = lax.broadcasted_iota(jnp.int32, (rows, LANES), 1)
    part = lane // head_dim

    def stack(values, target):
        for group in range(groups):
            block = values[:, group * LANES : (group + 1) * LANES]
            for index in range(per):
                target[group, index * rows : (index + 1) * rows, :] = jnp.where(
                    part == index, block, 0.0
                ).astype(BF16)

    def unstack(source):
        columns = []
        for group in range(groups):
            block = source[group, :rows, :]
            for index in range(1, per):
                block = jnp.where(
                    part == index, source[group, index * rows : (index + 1) * rows, :], block
                )
            columns.append(block)
        return jnp.concatenate(columns, axis=1)

    load_uq.wait()
    pre_uq = mul(rounded, wp[:, : 2 * att])
    pre_ref[:, : 2 * att] = pre_uq
    act_uq = pre_uq * sigmoid(pre_uq)
    gate_ref[...] = act_uq[:, :att].astype(BF16).astype(F32)
    stack(act_uq[:, att:] * score_scale, qs)
    load_go.wait()
    load_wo.wait()
    grad_gated = mul(go[...], wo[...], NT)

    chunk = 32

    @functools.partial(loop, 0, me + 1)
    def _(turn):
        block = me - turn

        @pl.when(turn > 0)
        def _():
            remote(
                st_all.at[block], st_all.at[block], st_send.at[block], st_recv.at[block],
                ctx_at(block),
            ).wait_recv()

        key_stamps = st_all[block][0:1, :]
        for first in range(0, rows, chunk):
            gap = scol[first : first + chunk, :] - key_stamps
            bucket = jnp.zeros(gap.shape, jnp.int32)
            bias = [jnp.full(gap.shape, steps[0, head], F32) for head in range(head_count)]
            for level in range(level_count - 1):
                above = gap >= (1 << level)
                bucket = jnp.where(above, level + 1, bucket)
                bias = [
                    jnp.where(above, steps[level + 1, head], bias[head])
                    for head in range(head_count)
                ]
            buckets[block, first : first + chunk, :] = bucket
            for head in range(head_count):
                start = (head % per) * rows + first
                sc[block, head // per, start : start + chunk, :] = bias[head]

    own_pos = me * rows + lax.broadcasted_iota(jnp.int32, (rows, LANES), 0)
    share = 1.0 / (jnp.minimum(own_pos, length - 1) + 1).astype(F32)
    mix[...] = jnp.zeros_like(mix)
    dq[...] = jnp.zeros_like(dq)

    @functools.partial(loop, 0, me + 1)
    def _(turn):
        block = me - turn

        @pl.when(turn > 0)
        def _():
            remote(
                kv_all.at[block], kv_all.at[block], kv_send.at[block], kv_recv.at[block],
                ctx_at(block),
            ).wait_recv()

        key_pos = block * rows + lane
        part_share = jnp.where((key_pos <= own_pos) & (key_pos < length), share, 0.0)
        shares = jnp.concatenate([part_share] * per, axis=0)
        for group in range(groups):
            keys = kv_all[block, :, group * LANES : (group + 1) * LANES]
            values = kv_all[block, :, att + group * LANES : att + (group + 1) * LANES]
            scores = mul(qs[group], keys, NT) + sc[block, group]
            sig = sigmoid(scores)
            shared = sig * shares
            weights = (scores * shared).astype(BF16)
            sc[block, group] = shared * (1.0 + scores * (1.0 - sig))
            wt[block, group] = weights
            mix[group] += mul(weights, values)

    mixed_norm, mixed_inv = norm_rows(unstack(mix))
    gate = gate_ref[...]
    grad_units = grad_gated * mixed_norm
    stack(norm_back(grad_gated * gate, mixed_norm, mixed_inv), gs)

    @functools.partial(loop, 0, me + 1)
    def _(block):
        for group in range(groups):
            low, high = group * LANES, (group + 1) * LANES
            keys = kv_all[block, :, low:high]
            values = kv_all[block, :, att + low : att + high]
            grad_scores = (mul(gs[group], values, NT) * sc[block, group]).astype(BF16)
            sc[block, group] = grad_scores.astype(F32)
            dq[group] += mul(grad_scores, keys)
            grad_k = mul(grad_scores, qs[group], TN)
            grad_val = mul(wt[block, group], gs[group], TN)
            own[:, low:high] = grad_k
            own[:, att + low : att + high] = grad_val
            snd[block, :, low:high] = grad_k.astype(BF16)
            snd[block, :, att + low : att + high] = grad_val.astype(BF16)

        @pl.when(block < me)
        def _():
            remote(
                snd.at[block], rcv.at[me], d_send.at[block], d_recv.at[me], ctx_at(block)
            ).start()

    tacc[...] = jnp.zeros_like(tacc)

    @functools.partial(loop, 0, me + 1)
    def _(block):
        bucket = buckets[block]
        for level in range(level_count):
            found = bucket == level
            for head in range(head_count):
                start = (head % per) * rows
                terms = jnp.where(found, sc[block, head // per, start : start + rows, :], 0.0)
                tacc[head, level] += jnp.sum(terms.reshape(rows // 8, 8, LANES), axis=0)

    table_lane = lax.broadcasted_iota(jnp.int32, (level_count, LANES), 1)
    local = jnp.zeros((level_count, LANES), F32)
    for head in range(head_count):
        summed = jnp.sum(jnp.sum(tacc[head], axis=1), axis=-1, keepdims=True)
        local = jnp.where(table_lane == head, summed, local)
    tab1[me] = local

    @functools.partial(loop, 1, ctx_count)
    def _(offset):
        rank = ctx_peer(offset)
        remote(
            tab1.at[me], tab1.at[me], t1_send.at[rank], t1_recv.at[me], ctx_at(rank)
        ).start()

    gated = (mixed_norm * gate).astype(BF16)
    layer_v[...] = (xv[...].astype(F32) + mul(gated, wo[...])).astype(BF16)
    write_layer = pltpu.make_async_copy(layer_v, layer_hbm, out_sem.at[0])
    write_layer.start()

    slope_uq = silu_slope(pre_ref[:, : 2 * att])
    grad_uq = jnp.concatenate([grad_units, unstack(dq) * score_scale], axis=1) * slope_uq
    grad_normed = mul(grad_uq.astype(BF16), wp[:, : 2 * att], NT)

    @functools.partial(loop, 1, ctx_count)
    def _(offset):
        rank = ctx_peer(offset)
        remote(
            tab1.at[rank], tab1.at[rank], t1_send.at[rank], t1_recv.at[rank], ctx_at(rank)
        ).wait_recv()

    group_sum = tab1[0]
    for rank in range(1, ctx_count):
        group_sum = group_sum + tab1[rank]
    tab2[my_dp] = group_sum

    @functools.partial(loop, 1, data_count)
    def _(offset):
        rank = dp_peer(offset)
        remote(
            tab2.at[my_dp], tab2.at[my_dp], t2_send.at[rank], t2_recv.at[my_dp], dp_at(rank)
        ).start()

    @functools.partial(loop, me + 1, ctx_count)
    def _(rank):
        remote(
            snd.at[rank], rcv.at[rank], d_send.at[rank], d_recv.at[rank], ctx_at(rank)
        ).wait_recv()
        own[...] += rcv[rank].astype(F32)

    grad_kv = own[...] * silu_slope(pre_ref[:, 2 * att :])
    grad_normed = grad_normed + mul(grad_kv.astype(BF16), wp[:, 2 * att :], NT)
    grad_v[...] = (
        norm_back(grad_normed, normed_ref[...], inverse) + go[...].astype(F32)
    ).astype(BF16)
    write_grad = pltpu.make_async_copy(grad_v, grad_hbm, out_sem.at[1])
    write_grad.start()

    @functools.partial(loop, 1, data_count)
    def _(offset):
        rank = dp_peer(offset)
        remote(
            tab2.at[rank], tab2.at[rank], t2_send.at[rank], t2_recv.at[rank], dp_at(rank)
        ).wait_recv()

    total = tab2[0]
    for rank in range(1, data_count):
        total = total + tab2[rank]
    gt_ref[...] = total[:, :head_count] * scale_table

    @functools.partial(loop, me + 1, ctx_count)
    def _(rank):
        remote(
            st_all.at[me], st_all.at[me], st_send.at[rank], st_recv.at[me], ctx_at(rank)
        ).wait_send()
        remote(
            kv_all.at[me], kv_all.at[me], kv_send.at[rank], kv_recv.at[me], ctx_at(rank)
        ).wait_send()

    @functools.partial(loop, 0, me)
    def _(block):
        remote(
            snd.at[block], rcv.at[me], d_send.at[block], d_recv.at[me], ctx_at(block)
        ).wait_send()

    @functools.partial(loop, 1, ctx_count)
    def _(offset):
        rank = ctx_peer(offset)
        remote(
            tab1.at[me], tab1.at[me], t1_send.at[rank], t1_recv.at[me], ctx_at(rank)
        ).wait_send()

    @functools.partial(loop, 1, data_count)
    def _(offset):
        rank = dp_peer(offset)
        remote(
            tab2.at[my_dp], tab2.at[my_dp], t2_send.at[rank], t2_recv.at[my_dp], dp_at(rank)
        ).wait_send()

    write_layer.wait()
    write_grad.wait()


def on_device(actions, stamps, lengths, w_proj, w_out, bias_table, grad_out):
    rows = actions.shape[1]
    model_dim = actions.shape[2]
    level_count, head_count = bias_table.shape
    att = w_out.shape[0]
    ctx_count = lax.axis_size("ctx")
    data_count = lax.axis_size("dp")
    groups = att // LANES
    per = LANES // (att // head_count)
    scale_table = 1.0 / math.sqrt(rows * ctx_count * data_count)
    vmem = pl.BlockSpec(memory_space=pltpu.VMEM)
    smem = pl.BlockSpec(memory_space=pltpu.SMEM)
    anywhere = pl.BlockSpec(memory_space=pl.ANY)
    dma = pltpu.SemaphoreType.DMA
    layer_rows, grad_rows, grad_table = pl.pallas_call(
        functools.partial(kernel, ctx_count, data_count, head_count, level_count, scale_table),
        out_shape=(
            jax.ShapeDtypeStruct((rows, model_dim), BF16),
            jax.ShapeDtypeStruct((rows, model_dim), BF16),
            jax.ShapeDtypeStruct((level_count, head_count), F32),
        ),
        in_specs=[smem, smem, vmem, anywhere, anywhere, anywhere, anywhere],
        out_specs=(anywhere, anywhere, vmem),
        scratch_shapes=[
            pltpu.VMEM((rows, model_dim), BF16),
            pltpu.VMEM((model_dim, 4 * att), BF16),
            pltpu.VMEM((att, model_dim), BF16),
            pltpu.VMEM((rows, model_dim), BF16),
            pltpu.VMEM((rows, model_dim), F32),
            pltpu.VMEM((rows, 4 * att), F32),
            pltpu.VMEM((rows, att), F32),
            pltpu.VMEM((ctx_count, rows, 2 * att), BF16),
            pltpu.VMEM((ctx_count, 8, LANES), jnp.int32),
            pltpu.VMEM((rows, LANES), jnp.int32),
            pltpu.SMEM((level_count, head_count), F32),
            pltpu.VMEM((groups, per * rows, LANES), BF16),
            pltpu.VMEM((groups, per * rows, LANES), BF16),
            pltpu.VMEM((ctx_count, rows, LANES), jnp.int32),
            pltpu.VMEM((ctx_count, groups, per * rows, LANES), F32),
            pltpu.VMEM((ctx_count, groups, per * rows, LANES), BF16),
            pltpu.VMEM((groups, per * rows, LANES), F32),
            pltpu.VMEM((groups, per * rows, LANES), F32),
            pltpu.VMEM((rows, 2 * att), F32),
            pltpu.VMEM((ctx_count, rows, 2 * att), BF16),
            pltpu.VMEM((ctx_count, rows, 2 * att), BF16),
            pltpu.VMEM((ctx_count, level_count, LANES), F32),
            pltpu.VMEM((data_count, level_count, LANES), F32),
            pltpu.VMEM((head_count, level_count, 8, LANES), F32),
            pltpu.VMEM((rows, model_dim), BF16),
            pltpu.VMEM((rows, model_dim), BF16),
            dma((5,)),
            dma((2,)),
            dma((ctx_count,)),
            dma((ctx_count,)),
            dma((ctx_count,)),
            dma((ctx_count,)),
            dma((ctx_count,)),
            dma((ctx_count,)),
            dma((ctx_count,)),
            dma((ctx_count,)),
            dma((data_count,)),
            dma((data_count,)),
        ],
        compiler_params=pltpu.CompilerParams(
            collective_id=0, has_side_effects=True, vmem_limit_bytes=48 * 1024 * 1024
        ),
    )(
        lengths,
        bias_table,
        stamps,
        actions.reshape(rows, model_dim),
        w_proj,
        w_out,
        grad_out.reshape(rows, model_dim),
    )
    return (
        layer_rows.reshape(1, rows, model_dim),
        grad_rows.reshape(1, rows, model_dim),
        grad_table,
    )


def solution(mesh):
    in_specs = (P("dp", "ctx", None), P("dp", "ctx"), P("dp"), P(), P(), P(), P("dp", "ctx", None))
    out_specs = (P("dp", "ctx", None), P("dp", "ctx", None), P())
    return jax.shard_map(
        on_device, mesh=mesh, in_specs=in_specs, out_specs=out_specs, check_vma=False
    )
```

```python
import functools
import math

import jax
import jax.numpy as jnp
from jax import lax
from jax.experimental import pallas as pl
from jax.experimental.pallas import tpu as pltpu
from jax.sharding import PartitionSpec as P

EPS = 1e-05
MESH = pl.DeviceIdType.MESH
LANES = 128
F32 = jnp.float32
BF16 = jnp.bfloat16
NT = (((1,), (1,)), ((), ()))
TN = (((0,), (0,)), ((), ()))
NN = (((1,), (0,)), ((), ()))


def mul(left, right, dims=NN):
    return lax.dot_general(left, right, dims, preferred_element_type=F32)


def sigmoid(values):
    return 0.5 * jnp.tanh(0.5 * values) + 0.5


def norm_rows(values):
    row_mean = jnp.mean(values, axis=-1, keepdims=True)
    centred = values - row_mean
    spread = jnp.mean(centred * centred, axis=-1, keepdims=True)
    inverse = lax.rsqrt(spread + EPS)
    return centred * inverse, inverse


def norm_back(incoming, normed, inverse):
    first = jnp.mean(incoming, axis=-1, keepdims=True)
    second = jnp.mean(incoming * normed, axis=-1, keepdims=True)
    return inverse * (incoming - first - normed * second)


def silu_slope(values):
    sig = sigmoid(values)
    return sig * (1.0 + values * (1.0 - sig))


def kernel(
    ctx_count, data_count, head_count, level_count, scale_table,
    len_ref, table_ref, stamps_hbm, x_hbm, wp_hbm, wo_hbm, go_hbm,
    layer_v, grad_v, gt_ref,
    stamps_ref, xv, wp, wo, go, normed_ref, pre_ref, gate_ref, kv_all, st_all, scol, steps,
    qs, gs, buckets, sc, wt, mix, dq, own, snd, rcv, tab1, tab2, tacc,
    load_sem, st_send, st_recv, kv_send, kv_recv, d_send, d_recv,
    t1_send, t1_recv, t2_send, t2_recv,
):
    rows, model_dim = xv.shape
    att = wo.shape[0]
    head_dim = att // head_count
    per = LANES // head_dim
    groups = att // LANES
    score_scale = head_dim ** (-0.5)
    me = lax.axis_index("ctx")
    my_dp = lax.axis_index("dp")
    ctx_at = lambda rank: {"ctx": rank}
    dp_at = lambda rank: {"dp": rank}

    def remote(src, dst, send_sem, recv_sem, where):
        return pltpu.make_async_remote_copy(
            src_ref=src, dst_ref=dst, send_sem=send_sem, recv_sem=recv_sem,
            device_id=where, device_id_type=MESH,
        )

    def loop(low, high, body):
        def step(index, carry):
            body(index)
            return carry

        lax.fori_loop(low, high, step, 0)

    load_x = pltpu.make_async_copy(x_hbm, xv, load_sem.at[0])
    load_kv = pltpu.make_async_copy(
        wp_hbm.at[:, pl.ds(2 * att, 2 * att)], wp.at[:, pl.ds(2 * att, 2 * att)], load_sem.at[1]
    )
    load_uq = pltpu.make_async_copy(
        wp_hbm.at[:, pl.ds(0, 2 * att)], wp.at[:, pl.ds(0, 2 * att)], load_sem.at[2]
    )
    load_go = pltpu.make_async_copy(go_hbm, go, load_sem.at[3])
    load_wo = pltpu.make_async_copy(wo_hbm, wo, load_sem.at[4])
    load_st = pltpu.make_async_copy(stamps_hbm, stamps_ref, load_sem.at[5])
    for load in (load_st, load_x, load_kv, load_uq, load_go, load_wo):
        load.start()

    barrier = pltpu.get_barrier_semaphore()
    ctx_peer = lambda offset: lax.rem(me + offset, ctx_count)
    dp_peer = lambda offset: lax.rem(my_dp + offset, data_count)

    @functools.partial(loop, 1, ctx_count)
    def _(offset):
        pl.semaphore_signal(
            barrier, inc=1, device_id=ctx_at(ctx_peer(offset)), device_id_type=MESH
        )

    @functools.partial(loop, 1, data_count)
    def _(offset):
        pl.semaphore_signal(
            barrier, inc=1, device_id=dp_at(dp_peer(offset)), device_id_type=MESH
        )

    length = len_ref[0]
    for head in range(head_count):
        running = table_ref[head, 0]
        steps[0, head] = running
        for level in range(level_count - 1):
            running = running + (table_ref[head, level + 1] - table_ref[head, level])
            steps[level + 1, head] = running

    load_st.wait()
    stamp_row = stamps_ref[...]
    st_all[me] = jnp.broadcast_to(stamp_row, (8, LANES))
    scol[...] = jnp.broadcast_to(stamp_row, (rows, LANES)).T

    load_x.wait()
    normed, inverse = norm_rows(xv[...].astype(F32))
    normed_ref[...] = normed
    rounded = normed.astype(BF16)
    load_kv.wait()
    pre_kv = mul(rounded, wp[:, 2 * att :])
    pre_ref[:, 2 * att :] = pre_kv
    kv_all[me] = (pre_kv * sigmoid(pre_kv)).astype(BF16)

    pl.semaphore_wait(barrier, ctx_count - 1 + data_count - 1)

    @functools.partial(loop, me + 1, ctx_count)
    def _(rank):
        remote(
            st_all.at[me], st_all.at[me], st_send.at[rank], st_recv.at[me], ctx_at(rank)
        ).start()

    @functools.partial(loop, me + 1, ctx_count)
    def _(rank):
        remote(
            kv_all.at[me], kv_all.at[me], kv_send.at[rank], kv_recv.at[me], ctx_at(rank)
        ).start()

    lane = lax.broadcasted_iota(jnp.int32, (rows, LANES), 1)
    part = lane // head_dim

    def stack(values, target):
        for group in range(groups):
            block = values[:, group * LANES : (group + 1) * LANES]
            for index in range(per):
                target[group, index * rows : (index + 1) * rows, :] = jnp.where(
                    part == index, block, 0.0
                ).astype(BF16)

    def unstack(source):
        columns = []
        for group in range(groups):
            block = source[group, :rows, :]
            for index in range(1, per):
                block = jnp.where(
                    part == index, source[group, index * rows : (index + 1) * rows, :], block
                )
            columns.append(block)
        return jnp.concatenate(columns, axis=1)

    load_uq.wait()
    pre_uq = mul(rounded, wp[:, : 2 * att])
    pre_ref[:, : 2 * att] = pre_uq
    act_uq = pre_uq * sigmoid(pre_uq)
    gate_ref[...] = act_uq[:, :att].astype(BF16).astype(F32)
    stack(act_uq[:, att:] * score_scale, qs)
    load_go.wait()
    load_wo.wait()
    grad_gated = mul(go[...], wo[...], NT)

    chunk = 32

    @functools.partial(loop, 0, me + 1)
    def _(turn):
        block = me - turn

        @pl.when(turn > 0)
        def _():
            remote(
                st_all.at[block], st_all.at[block], st_send.at[block], st_recv.at[block],
                ctx_at(block),
            ).wait_recv()

        key_stamps = st_all[block][0:1, :]
        for first in range(0, rows, chunk):
            gap = scol[first : first + chunk, :] - key_stamps
            bucket = jnp.zeros(gap.shape, jnp.int32)
            bias = [jnp.full(gap.shape, steps[0, head], F32) for head in range(head_count)]
            for level in range(level_count - 1):
                above = gap >= (1 << level)
                bucket = jnp.where(above, level + 1, bucket)
                bias = [
                    jnp.where(above, steps[level + 1, head], bias[head])
                    for head in range(head_count)
                ]
            buckets[block, first : first + chunk, :] = bucket
            for head in range(head_count):
                start = (head % per) * rows + first
                sc[block, head // per, start : start + chunk, :] = bias[head]

    own_pos = me * rows + lax.broadcasted_iota(jnp.int32, (rows, LANES), 0)
    share = 1.0 / (jnp.minimum(own_pos, length - 1) + 1).astype(F32)
    mix[...] = jnp.zeros_like(mix)
    dq[...] = jnp.zeros_like(dq)

    @functools.partial(loop, 0, me + 1)
    def _(turn):
        block = me - turn

        @pl.when(turn > 0)
        def _():
            remote(
                kv_all.at[block], kv_all.at[block], kv_send.at[block], kv_recv.at[block],
                ctx_at(block),
            ).wait_recv()

        key_pos = block * rows + lane
        part_share = jnp.where((key_pos <= own_pos) & (key_pos < length), share, 0.0)
        shares = jnp.concatenate([part_share] * per, axis=0)
        for group in range(groups):
            keys = kv_all[block, :, group * LANES : (group + 1) * LANES]
            values = kv_all[block, :, att + group * LANES : att + (group + 1) * LANES]
            scores = mul(qs[group], keys, NT) + sc[block, group]
            sig = sigmoid(scores)
            shared = sig * shares
            weights = (scores * shared).astype(BF16)
            sc[block, group] = shared * (1.0 + scores * (1.0 - sig))
            wt[block, group] = weights
            mix[group] += mul(weights, values)

    mixed_norm, mixed_inv = norm_rows(unstack(mix))
    gate = gate_ref[...]
    grad_units = grad_gated * mixed_norm
    stack(norm_back(grad_gated * gate, mixed_norm, mixed_inv), gs)

    @functools.partial(loop, 0, me + 1)
    def _(block):
        for group in range(groups):
            low, high = group * LANES, (group + 1) * LANES
            keys = kv_all[block, :, low:high]
            values = kv_all[block, :, att + low : att + high]
            grad_scores = (mul(gs[group], values, NT) * sc[block, group]).astype(BF16)
            sc[block, group] = grad_scores.astype(F32)
            dq[group] += mul(grad_scores, keys)
            grad_k = mul(grad_scores, qs[group], TN)
            grad_val = mul(wt[block, group], gs[group], TN)
            own[:, low:high] = grad_k
            own[:, att + low : att + high] = grad_val
            snd[block, :, low:high] = grad_k.astype(BF16)
            snd[block, :, att + low : att + high] = grad_val.astype(BF16)

        @pl.when(block < me)
        def _():
            remote(
                snd.at[block], rcv.at[me], d_send.at[block], d_recv.at[me], ctx_at(block)
            ).start()

    tacc[...] = jnp.zeros_like(tacc)

    @functools.partial(loop, 0, me + 1)
    def _(block):
        bucket = buckets[block]
        for level in range(level_count):
            found = bucket == level
            for head in range(head_count):
                start = (head % per) * rows
                terms = jnp.where(found, sc[block, head // per, start : start + rows, :], 0.0)
                tacc[head, level] += jnp.sum(terms.reshape(rows // 8, 8, LANES), axis=0)

    cells = head_count * level_count
    summed = jnp.concatenate(
        [
            jnp.sum(tacc[...], axis=2).reshape(cells, LANES),
            jnp.zeros((LANES - cells, LANES), F32),
        ],
        axis=0,
    )
    local = jnp.broadcast_to(jnp.sum(summed.T, axis=0, keepdims=True), (8, LANES))
    tab1[me] = local

    @functools.partial(loop, 1, ctx_count)
    def _(offset):
        rank = ctx_peer(offset)
        remote(
            tab1.at[me], tab1.at[me], t1_send.at[rank], t1_recv.at[me], ctx_at(rank)
        ).start()

    gated = (mixed_norm * gate).astype(BF16)
    layer_v[...] = (xv[...].astype(F32) + mul(gated, wo[...])).astype(BF16)

    slope_uq = silu_slope(pre_ref[:, : 2 * att])
    grad_uq = jnp.concatenate([grad_units, unstack(dq) * score_scale], axis=1) * slope_uq
    grad_normed = mul(grad_uq.astype(BF16), wp[:, : 2 * att], NT)

    @functools.partial(loop, 1, ctx_count)
    def _(offset):
        rank = ctx_peer(offset)
        remote(
            tab1.at[rank], tab1.at[rank], t1_send.at[rank], t1_recv.at[rank], ctx_at(rank)
        ).wait_recv()

    group_sum = tab1[0]
    for rank in range(1, ctx_count):
        group_sum = group_sum + tab1[rank]
    tab2[my_dp] = group_sum

    @functools.partial(loop, 1, data_count)
    def _(offset):
        rank = dp_peer(offset)
        remote(
            tab2.at[my_dp], tab2.at[my_dp], t2_send.at[rank], t2_recv.at[my_dp], dp_at(rank)
        ).start()

    @functools.partial(loop, me + 1, ctx_count)
    def _(rank):
        remote(
            snd.at[rank], rcv.at[rank], d_send.at[rank], d_recv.at[rank], ctx_at(rank)
        ).wait_recv()
        own[...] += rcv[rank].astype(F32)

    grad_kv = own[...] * silu_slope(pre_ref[:, 2 * att :])
    grad_normed = grad_normed + mul(grad_kv.astype(BF16), wp[:, 2 * att :], NT)
    grad_v[...] = (
        norm_back(grad_normed, normed_ref[...], inverse) + go[...].astype(F32)
    ).astype(BF16)

    @functools.partial(loop, 1, data_count)
    def _(offset):
        rank = dp_peer(offset)
        remote(
            tab2.at[rank], tab2.at[rank], t2_send.at[rank], t2_recv.at[rank], dp_at(rank)
        ).wait_recv()

    total = tab2[0]
    for rank in range(1, data_count):
        total = total + tab2[rank]
    for head in range(head_count):
        cells = total[0:1, head * level_count : (head + 1) * level_count]
        gt_ref[head : head + 1, :] = cells * scale_table

    @functools.partial(loop, me + 1, ctx_count)
    def _(rank):
        remote(
            st_all.at[me], st_all.at[me], st_send.at[rank], st_recv.at[me], ctx_at(rank)
        ).wait_send()
        remote(
            kv_all.at[me], kv_all.at[me], kv_send.at[rank], kv_recv.at[me], ctx_at(rank)
        ).wait_send()

    @functools.partial(loop, 0, me)
    def _(block):
        remote(
            snd.at[block], rcv.at[me], d_send.at[block], d_recv.at[me], ctx_at(block)
        ).wait_send()

    @functools.partial(loop, 1, ctx_count)
    def _(offset):
        rank = ctx_peer(offset)
        remote(
            tab1.at[me], tab1.at[me], t1_send.at[rank], t1_recv.at[me], ctx_at(rank)
        ).wait_send()

    @functools.partial(loop, 1, data_count)
    def _(offset):
        rank = dp_peer(offset)
        remote(
            tab2.at[my_dp], tab2.at[my_dp], t2_send.at[rank], t2_recv.at[my_dp], dp_at(rank)
        ).wait_send()


def on_device(actions, stamps, lengths, w_proj, w_out, bias_table, grad_out):
    rows = actions.shape[1]
    model_dim = actions.shape[2]
    level_count, head_count = bias_table.shape
    att = w_out.shape[0]
    ctx_count = lax.axis_size("ctx")
    data_count = lax.axis_size("dp")
    groups = att // LANES
    per = LANES // (att // head_count)
    scale_table = 1.0 / math.sqrt(rows * ctx_count * data_count)
    vmem = pl.BlockSpec(memory_space=pltpu.VMEM)
    smem = pl.BlockSpec(memory_space=pltpu.SMEM)
    anywhere = pl.BlockSpec(memory_space=pltpu.HBM)
    dma = pltpu.SemaphoreType.DMA
    layer_rows, grad_rows, grad_table = pl.pallas_call(
        functools.partial(kernel, ctx_count, data_count, head_count, level_count, scale_table),
        out_shape=(
            jax.ShapeDtypeStruct((rows, model_dim), BF16),
            jax.ShapeDtypeStruct((rows, model_dim), BF16),
            jax.ShapeDtypeStruct((head_count, level_count), F32),
        ),
        in_specs=[smem, smem, anywhere, anywhere, anywhere, anywhere, anywhere],
        out_specs=(vmem, vmem, vmem),
        scratch_shapes=[
            pltpu.VMEM((1, rows), jnp.int32),
            pltpu.VMEM((rows, model_dim), BF16),
            pltpu.VMEM((model_dim, 4 * att), BF16),
            pltpu.VMEM((att, model_dim), BF16),
            pltpu.VMEM((rows, model_dim), BF16),
            pltpu.VMEM((rows, model_dim), F32),
            pltpu.VMEM((rows, 4 * att), F32),
            pltpu.VMEM((rows, att), F32),
            pltpu.VMEM((ctx_count, rows, 2 * att), BF16),
            pltpu.VMEM((ctx_count, 8, LANES), jnp.int32),
            pltpu.VMEM((rows, LANES), jnp.int32),
            pltpu.SMEM((level_count, head_count), F32),
            pltpu.VMEM((groups, per * rows, LANES), BF16),
            pltpu.VMEM((groups, per * rows, LANES), BF16),
            pltpu.VMEM((ctx_count, rows, LANES), jnp.int32),
            pltpu.VMEM((ctx_count, groups, per * rows, LANES), F32),
            pltpu.VMEM((ctx_count, groups, per * rows, LANES), BF16),
            pltpu.VMEM((groups, per * rows, LANES), F32),
            pltpu.VMEM((groups, per * rows, LANES), F32),
            pltpu.VMEM((rows, 2 * att), F32),
            pltpu.VMEM((ctx_count, rows, 2 * att), BF16),
            pltpu.VMEM((ctx_count, rows, 2 * att), BF16),
            pltpu.VMEM((ctx_count, 8, LANES), F32),
            pltpu.VMEM((data_count, 8, LANES), F32),
            pltpu.VMEM((head_count, level_count, 8, LANES), F32),
            dma((6,)),
            dma((ctx_count,)),
            dma((ctx_count,)),
            dma((ctx_count,)),
            dma((ctx_count,)),
            dma((ctx_count,)),
            dma((ctx_count,)),
            dma((ctx_count,)),
            dma((ctx_count,)),
            dma((data_count,)),
            dma((data_count,)),
        ],
        compiler_params=pltpu.CompilerParams(
            collective_id=0, has_side_effects=True, vmem_limit_bytes=60 * 1024 * 1024
        ),
    )(
        lengths,
        bias_table.T,
        stamps,
        actions.reshape(rows, model_dim),
        w_proj,
        w_out,
        grad_out.reshape(rows, model_dim),
    )
    return (
        layer_rows.reshape(1, rows, model_dim),
        grad_rows.reshape(1, rows, model_dim),
        grad_table.T,
    )


def solution(mesh):
    in_specs = (P("dp", "ctx", None), P("dp", "ctx"), P("dp"), P(), P(), P(), P("dp", "ctx", None))
    out_specs = (P("dp", "ctx", None), P("dp", "ctx", None), P())
    return jax.shard_map(
        on_device, mesh=mesh, in_specs=in_specs, out_specs=out_specs, check_vma=False
    )
```

```python
import functools
import math

import jax
import jax.numpy as jnp
from jax import lax
from jax.experimental import pallas as pl
from jax.experimental.pallas import tpu as pltpu
from jax.sharding import PartitionSpec as P

EPS = 1e-05
MESH = pl.DeviceIdType.MESH
LANES = 128
F32 = jnp.float32
BF16 = jnp.bfloat16
NT = (((1,), (1,)), ((), ()))
TN = (((0,), (0,)), ((), ()))
NN = (((1,), (0,)), ((), ()))


def mul(left, right, dims=NN):
    return lax.dot_general(left, right, dims, preferred_element_type=F32)


def sigmoid(values):
    return 0.5 * jnp.tanh(0.5 * values) + 0.5


def norm_rows(values):
    row_mean = jnp.mean(values, axis=-1, keepdims=True)
    centred = values - row_mean
    spread = jnp.mean(centred * centred, axis=-1, keepdims=True)
    inverse = lax.rsqrt(spread + EPS)
    return centred * inverse, inverse


def norm_back(incoming, normed, inverse):
    first = jnp.mean(incoming, axis=-1, keepdims=True)
    second = jnp.mean(incoming * normed, axis=-1, keepdims=True)
    return inverse * (incoming - first - normed * second)


def silu_slope(values):
    sig = sigmoid(values)
    return sig * (1.0 + values * (1.0 - sig))


def kernel(
    ctx_count, data_count, head_count, level_count, scale_table,
    len_ref, table_ref, stamps_hbm, x_hbm, wp_hbm, wo_hbm, go_hbm,
    layer_hbm, grad_hbm, gt_ref,
    stamps_ref, xv, wp, wo, go, normed_ref, pre_ref, gate_ref, kv_all, st_all, scol, steps,
    q_all, g_all, qs, gs, buckets, sc, wt, mix, dq, own, tab1, tab2, tacc, layer_v, grad_v,
    load_sem, out_sem, st_send, st_recv, kv_send, kv_recv, q_send, q_recv, g_send, g_recv,
    t1_send, t1_recv, t2_send, t2_recv,
):
    rows, model_dim = xv.shape
    att = wo.shape[0]
    head_dim = att // head_count
    per = LANES // head_dim
    groups = att // LANES
    score_scale = head_dim ** (-0.5)
    me = lax.axis_index("ctx")
    my_dp = lax.axis_index("dp")
    ctx_at = lambda rank: {"ctx": rank}
    dp_at = lambda rank: {"dp": rank}

    def remote(src, dst, send_sem, recv_sem, where):
        return pltpu.make_async_remote_copy(
            src_ref=src, dst_ref=dst, send_sem=send_sem, recv_sem=recv_sem,
            device_id=where, device_id_type=MESH,
        )

    def loop(low, high, body):
        def step(index, carry):
            body(index)
            return carry

        lax.fori_loop(low, high, step, 0)

    load_x = pltpu.make_async_copy(x_hbm, xv, load_sem.at[0])
    load_kv = pltpu.make_async_copy(
        wp_hbm.at[:, pl.ds(2 * att, 2 * att)], wp.at[:, pl.ds(2 * att, 2 * att)], load_sem.at[1]
    )
    load_uq = pltpu.make_async_copy(
        wp_hbm.at[:, pl.ds(0, 2 * att)], wp.at[:, pl.ds(0, 2 * att)], load_sem.at[2]
    )
    load_go = pltpu.make_async_copy(go_hbm, go, load_sem.at[3])
    load_wo = pltpu.make_async_copy(wo_hbm, wo, load_sem.at[4])
    load_st = pltpu.make_async_copy(stamps_hbm, stamps_ref, load_sem.at[5])
    for load in (load_st, load_x, load_kv, load_uq, load_go, load_wo):
        load.start()

    barrier = pltpu.get_barrier_semaphore()
    ctx_peer = lambda offset: lax.rem(me + offset, ctx_count)
    dp_peer = lambda offset: lax.rem(my_dp + offset, data_count)

    @functools.partial(loop, 1, ctx_count)
    def _(offset):
        pl.semaphore_signal(
            barrier, inc=1, device_id=ctx_at(ctx_peer(offset)), device_id_type=MESH
        )

    @functools.partial(loop, 1, data_count)
    def _(offset):
        pl.semaphore_signal(
            barrier, inc=1, device_id=dp_at(dp_peer(offset)), device_id_type=MESH
        )

    length = len_ref[0]
    for head in range(head_count):
        running = table_ref[head, 0]
        steps[0, head] = running
        for level in range(level_count - 1):
            running = running + (table_ref[head, level + 1] - table_ref[head, level])
            steps[level + 1, head] = running

    load_st.wait()
    stamp_row = stamps_ref[...]
    st_all[me] = jnp.broadcast_to(stamp_row, (8, LANES))
    scol[...] = jnp.broadcast_to(stamp_row, (rows, LANES)).T

    load_x.wait()
    normed, inverse = norm_rows(xv[...].astype(F32))
    normed_ref[...] = normed
    rounded = normed.astype(BF16)
    load_kv.wait()
    pre_kv = mul(rounded, wp[:, 2 * att :])
    pre_ref[:, 2 * att :] = pre_kv
    kv_all[me] = (pre_kv * sigmoid(pre_kv)).astype(BF16)

    pl.semaphore_wait(barrier, ctx_count - 1 + data_count - 1)

    @functools.partial(loop, 1, ctx_count)
    def _(offset):
        rank = ctx_peer(offset)
        remote(
            st_all.at[me], st_all.at[me], st_send.at[rank], st_recv.at[me], ctx_at(rank)
        ).start()

    @functools.partial(loop, me + 1, ctx_count)
    def _(rank):
        remote(
            kv_all.at[me], kv_all.at[me], kv_send.at[rank], kv_recv.at[me], ctx_at(rank)
        ).start()

    lane = lax.broadcasted_iota(jnp.int32, (rows, LANES), 1)
    part = lane // head_dim

    def stack(values, target, slot):
        for group in range(groups):
            block = values[:, group * LANES : (group + 1) * LANES]
            for index in range(per):
                target[slot, group, index * rows : (index + 1) * rows, :] = jnp.where(
                    part == index, block, 0.0
                ).astype(BF16)

    def unstack(source):
        columns = []
        for group in range(groups):
            block = source[group, :rows, :]
            for index in range(1, per):
                block = jnp.where(
                    part == index, source[group, index * rows : (index + 1) * rows, :], block
                )
            columns.append(block)
        return jnp.concatenate(columns, axis=1)

    load_uq.wait()
    pre_uq = mul(rounded, wp[:, : 2 * att])
    pre_ref[:, : 2 * att] = pre_uq
    act_uq = pre_uq * sigmoid(pre_uq)
    gate_ref[...] = act_uq[:, :att].astype(BF16).astype(F32)
    own_q = act_uq[:, att:] * score_scale
    q_all[me] = own_q.astype(BF16)

    @functools.partial(loop, 0, me)
    def _(rank):
        remote(
            q_all.at[me], q_all.at[me], q_send.at[rank], q_recv.at[me], ctx_at(rank)
        ).start()

    stack(own_q, qs, me)
    load_go.wait()
    load_wo.wait()
    grad_gated = mul(go[...], wo[...], NT)

    chunk = 32

    def add_bias(block, columns, key_stamps):
        for first in range(0, rows, chunk):
            gap = columns[first : first + chunk, :] - key_stamps
            bucket = jnp.zeros(gap.shape, jnp.int32)
            bias = [jnp.full(gap.shape, steps[0, head], F32) for head in range(head_count)]
            for level in range(level_count - 1):
                above = gap >= (1 << level)
                bucket = jnp.where(above, level + 1, bucket)
                bias = [
                    jnp.where(above, steps[level + 1, head], bias[head])
                    for head in range(head_count)
                ]
            buckets[block, first : first + chunk, :] = bucket
            for head in range(head_count):
                start = (head % per) * rows + first
                sc[block, head // per, start : start + chunk, :] = bias[head]

    def wait_stamps(rank):
        remote(
            st_all.at[rank], st_all.at[rank], st_send.at[rank], st_recv.at[rank], ctx_at(rank)
        ).wait_recv()

    @functools.partial(loop, 0, me + 1)
    def _(turn):
        block = me - turn

        @pl.when(turn > 0)
        def _():
            wait_stamps(block)

        add_bias(block, scol[...], st_all[block][0:1, :])

    def score_block(block, query_at, first_query, first_key, keys_at):
        query_pos = first_query * rows + lax.broadcasted_iota(jnp.int32, (rows, LANES), 0)
        share = 1.0 / (jnp.minimum(query_pos, length - 1) + 1).astype(F32)
        key_pos = first_key * rows + lane
        part_share = jnp.where((key_pos <= query_pos) & (key_pos < length), share, 0.0)
        shares = jnp.concatenate([part_share] * per, axis=0)
        for group in range(groups):
            keys = kv_all[keys_at, :, group * LANES : (group + 1) * LANES]
            scores = mul(qs[query_at, group], keys, NT) + sc[block, group]
            sig = sigmoid(scores)
            shared = sig * shares
            sc[block, group] = shared * (1.0 + scores * (1.0 - sig))
            wt[block, group] = (scores * shared).astype(BF16)

    mix[...] = jnp.zeros_like(mix)
    dq[...] = jnp.zeros_like(dq)

    @functools.partial(loop, 0, me + 1)
    def _(turn):
        block = me - turn

        @pl.when(turn > 0)
        def _():
            remote(
                kv_all.at[block], kv_all.at[block], kv_send.at[block], kv_recv.at[block],
                ctx_at(block),
            ).wait_recv()

        score_block(block, me, me, block, block)
        for group in range(groups):
            values = kv_all[block, :, att + group * LANES : att + (group + 1) * LANES]
            mix[group] += mul(wt[block, group], values)

    mixed_norm, mixed_inv = norm_rows(unstack(mix))
    gate = gate_ref[...]
    grad_units = grad_gated * mixed_norm
    own_g = norm_back(grad_gated * gate, mixed_norm, mixed_inv)
    g_all[me] = own_g.astype(BF16)

    @functools.partial(loop, 0, me)
    def _(rank):
        remote(
            g_all.at[me], g_all.at[me], g_send.at[rank], g_recv.at[me], ctx_at(rank)
        ).start()

    stack(own_g, gs, me)

    @functools.partial(loop, me + 1, ctx_count)
    def _(block):
        wait_stamps(block)
        stamp_block = jnp.broadcast_to(st_all[block][0:1, :], (rows, LANES))
        add_bias(block, stamp_block.T, st_all[me][0:1, :])
        remote(
            q_all.at[block], q_all.at[block], q_send.at[block], q_recv.at[block], ctx_at(block)
        ).wait_recv()
        stack(q_all[block].astype(F32), qs, block)
        score_block(block, block, block, me, me)

    def back_scores(block, query_at, keys_at, group):
        values = kv_all[keys_at, :, att + group * LANES : att + (group + 1) * LANES]
        return (mul(gs[query_at, group], values, NT) * sc[block, group]).astype(BF16)

    def add_key_grads(block, group, grad_scores):
        low, high = group * LANES, (group + 1) * LANES
        own[:, low:high] += mul(grad_scores, qs[block, group], TN)
        own[:, att + low : att + high] += mul(wt[block, group], gs[block, group], TN)

    own[...] = jnp.zeros_like(own)

    @functools.partial(loop, 0, me + 1)
    def _(block):
        for group in range(groups):
            keys = kv_all[block, :, group * LANES : (group + 1) * LANES]
            grad_scores = back_scores(block, me, block, group)
            sc[block, group] = grad_scores.astype(F32)
            dq[group] += mul(grad_scores, keys)

            @pl.when(block == me)
            def _():
                add_key_grads(block, group, grad_scores)

    tacc[...] = jnp.zeros_like(tacc)

    @functools.partial(loop, 0, me + 1)
    def _(block):
        bucket = buckets[block]
        for level in range(level_count):
            found = bucket == level
            for head in range(head_count):
                start = (head % per) * rows
                terms = jnp.where(found, sc[block, head // per, start : start + rows, :], 0.0)
                tacc[head, level] += jnp.sum(terms.reshape(rows // 8, 8, LANES), axis=0)

    cells = head_count * level_count
    summed = jnp.concatenate(
        [
            jnp.sum(tacc[...], axis=2).reshape(cells, LANES),
            jnp.zeros((LANES - cells, LANES), F32),
        ],
        axis=0,
    )
    local = jnp.broadcast_to(jnp.sum(summed.T, axis=0, keepdims=True), (8, LANES))
    tab1[me] = local

    @functools.partial(loop, 1, ctx_count)
    def _(offset):
        rank = ctx_peer(offset)
        remote(
            tab1.at[me], tab1.at[me], t1_send.at[rank], t1_recv.at[me], ctx_at(rank)
        ).start()

    gated = (mixed_norm * gate).astype(BF16)
    layer_v[...] = (xv[...].astype(F32) + mul(gated, wo[...])).astype(BF16)
    write_layer = pltpu.make_async_copy(layer_v, layer_hbm, out_sem.at[0])
    write_layer.start()

    slope_uq = silu_slope(pre_ref[:, : 2 * att])
    grad_uq = jnp.concatenate([grad_units, unstack(dq) * score_scale], axis=1) * slope_uq
    grad_normed = mul(grad_uq.astype(BF16), wp[:, : 2 * att], NT)

    @functools.partial(loop, 1, ctx_count)
    def _(offset):
        rank = ctx_peer(offset)
        remote(
            tab1.at[rank], tab1.at[rank], t1_send.at[rank], t1_recv.at[rank], ctx_at(rank)
        ).wait_recv()

    group_sum = tab1[0]
    for rank in range(1, ctx_count):
        group_sum = group_sum + tab1[rank]
    tab2[my_dp] = group_sum

    @functools.partial(loop, 1, data_count)
    def _(offset):
        rank = dp_peer(offset)
        remote(
            tab2.at[my_dp], tab2.at[my_dp], t2_send.at[rank], t2_recv.at[my_dp], dp_at(rank)
        ).start()

    @functools.partial(loop, me + 1, ctx_count)
    def _(rank):
        remote(
            g_all.at[rank], g_all.at[rank], g_send.at[rank], g_recv.at[rank], ctx_at(rank)
        ).wait_recv()
        stack(g_all[rank].astype(F32), gs, rank)
        for group in range(groups):
            add_key_grads(rank, group, back_scores(rank, rank, me, group))

    grad_kv = own[...] * silu_slope(pre_ref[:, 2 * att :])
    grad_normed = grad_normed + mul(grad_kv.astype(BF16), wp[:, 2 * att :], NT)
    grad_v[...] = (
        norm_back(grad_normed, normed_ref[...], inverse) + go[...].astype(F32)
    ).astype(BF16)
    write_grad = pltpu.make_async_copy(grad_v, grad_hbm, out_sem.at[1])
    write_grad.start()

    @functools.partial(loop, 1, data_count)
    def _(offset):
        rank = dp_peer(offset)
        remote(
            tab2.at[rank], tab2.at[rank], t2_send.at[rank], t2_recv.at[rank], dp_at(rank)
        ).wait_recv()

    total = tab2[0]
    for rank in range(1, data_count):
        total = total + tab2[rank]
    for head in range(head_count):
        cells = total[0:1, head * level_count : (head + 1) * level_count]
        gt_ref[head : head + 1, :] = cells * scale_table

    @functools.partial(loop, me + 1, ctx_count)
    def _(rank):
        remote(
            kv_all.at[me], kv_all.at[me], kv_send.at[rank], kv_recv.at[me], ctx_at(rank)
        ).wait_send()

    @functools.partial(loop, 0, me)
    def _(block):
        remote(
            q_all.at[me], q_all.at[me], q_send.at[block], q_recv.at[me], ctx_at(block)
        ).wait_send()
        remote(
            g_all.at[me], g_all.at[me], g_send.at[block], g_recv.at[me], ctx_at(block)
        ).wait_send()

    @functools.partial(loop, 1, ctx_count)
    def _(offset):
        rank = ctx_peer(offset)
        remote(
            tab1.at[me], tab1.at[me], t1_send.at[rank], t1_recv.at[me], ctx_at(rank)
        ).wait_send()
        remote(
            st_all.at[me], st_all.at[me], st_send.at[rank], st_recv.at[me], ctx_at(rank)
        ).wait_send()

    @functools.partial(loop, 1, data_count)
    def _(offset):
        rank = dp_peer(offset)
        remote(
            tab2.at[my_dp], tab2.at[my_dp], t2_send.at[rank], t2_recv.at[my_dp], dp_at(rank)
        ).wait_send()

    write_layer.wait()
    write_grad.wait()


def on_device(actions, stamps, lengths, w_proj, w_out, bias_table, grad_out):
    rows = actions.shape[1]
    model_dim = actions.shape[2]
    level_count, head_count = bias_table.shape
    att = w_out.shape[0]
    ctx_count = lax.axis_size("ctx")
    data_count = lax.axis_size("dp")
    groups = att // LANES
    per = LANES // (att // head_count)
    scale_table = 1.0 / math.sqrt(rows * ctx_count * data_count)
    vmem = pl.BlockSpec(memory_space=pltpu.VMEM)
    smem = pl.BlockSpec(memory_space=pltpu.SMEM)
    anywhere = pl.BlockSpec(memory_space=pltpu.HBM)
    dma = pltpu.SemaphoreType.DMA
    layer_rows, grad_rows, grad_table = pl.pallas_call(
        functools.partial(kernel, ctx_count, data_count, head_count, level_count, scale_table),
        out_shape=(
            jax.ShapeDtypeStruct((rows, model_dim), BF16),
            jax.ShapeDtypeStruct((rows, model_dim), BF16),
            jax.ShapeDtypeStruct((head_count, level_count), F32),
        ),
        in_specs=[smem, smem, anywhere, anywhere, anywhere, anywhere, anywhere],
        out_specs=(anywhere, anywhere, vmem),
        scratch_shapes=[
            pltpu.VMEM((1, rows), jnp.int32),
            pltpu.VMEM((rows, model_dim), BF16),
            pltpu.VMEM((model_dim, 4 * att), BF16),
            pltpu.VMEM((att, model_dim), BF16),
            pltpu.VMEM((rows, model_dim), BF16),
            pltpu.VMEM((rows, model_dim), F32),
            pltpu.VMEM((rows, 4 * att), F32),
            pltpu.VMEM((rows, att), F32),
            pltpu.VMEM((ctx_count, rows, 2 * att), BF16),
            pltpu.VMEM((ctx_count, 8, LANES), jnp.int32),
            pltpu.VMEM((rows, LANES), jnp.int32),
            pltpu.SMEM((level_count, head_count), F32),
            pltpu.VMEM((ctx_count, rows, att), BF16),
            pltpu.VMEM((ctx_count, rows, att), BF16),
            pltpu.VMEM((ctx_count, groups, per * rows, LANES), BF16),
            pltpu.VMEM((ctx_count, groups, per * rows, LANES), BF16),
            pltpu.VMEM((ctx_count, rows, LANES), jnp.int32),
            pltpu.VMEM((ctx_count, groups, per * rows, LANES), F32),
            pltpu.VMEM((ctx_count, groups, per * rows, LANES), BF16),
            pltpu.VMEM((groups, per * rows, LANES), F32),
            pltpu.VMEM((groups, per * rows, LANES), F32),
            pltpu.VMEM((rows, 2 * att), F32),
            pltpu.VMEM((ctx_count, 8, LANES), F32),
            pltpu.VMEM((data_count, 8, LANES), F32),
            pltpu.VMEM((head_count, level_count, 8, LANES), F32),
            pltpu.VMEM((rows, model_dim), BF16),
            pltpu.VMEM((rows, model_dim), BF16),
            dma((6,)),
            dma((2,)),
            dma((ctx_count,)),
            dma((ctx_count,)),
            dma((ctx_count,)),
            dma((ctx_count,)),
            dma((ctx_count,)),
            dma((ctx_count,)),
            dma((ctx_count,)),
            dma((ctx_count,)),
            dma((ctx_count,)),
            dma((ctx_count,)),
            dma((data_count,)),
            dma((data_count,)),
        ],
        compiler_params=pltpu.CompilerParams(
            collective_id=0, has_side_effects=True, vmem_limit_bytes=60 * 1024 * 1024
        ),
    )(
        lengths,
        bias_table.T,
        stamps,
        actions.reshape(rows, model_dim),
        w_proj,
        w_out,
        grad_out.reshape(rows, model_dim),
    )
    return (
        layer_rows.reshape(1, rows, model_dim),
        grad_rows.reshape(1, rows, model_dim),
        grad_table.T,
    )


def solution(mesh):
    in_specs = (P("dp", "ctx", None), P("dp", "ctx"), P("dp"), P(), P(), P(), P("dp", "ctx", None))
    out_specs = (P("dp", "ctx", None), P("dp", "ctx", None), P())
    return jax.shard_map(
        on_device, mesh=mesh, in_specs=in_specs, out_specs=out_specs, check_vma=False
    )
```

```python
import functools
import math

import jax
import jax.numpy as jnp
from jax import lax
from jax.experimental import pallas as pl
from jax.experimental.pallas import tpu as pltpu
from jax.sharding import PartitionSpec as P

EPS = 1e-05
MESH = pl.DeviceIdType.MESH
LANES = 128
F32 = jnp.float32
BF16 = jnp.bfloat16
NT = (((1,), (1,)), ((), ()))
TN = (((0,), (0,)), ((), ()))
NN = (((1,), (0,)), ((), ()))


def mul(left, right, dims=NN):
    return lax.dot_general(left, right, dims, preferred_element_type=F32)


def sigmoid(values):
    return 0.5 * jnp.tanh(0.5 * values) + 0.5


def norm_rows(values):
    row_mean = jnp.mean(values, axis=-1, keepdims=True)
    centred = values - row_mean
    spread = jnp.mean(centred * centred, axis=-1, keepdims=True)
    inverse = lax.rsqrt(spread + EPS)
    return centred * inverse, inverse


def norm_back(incoming, normed, inverse):
    first = jnp.mean(incoming, axis=-1, keepdims=True)
    second = jnp.mean(incoming * normed, axis=-1, keepdims=True)
    return inverse * (incoming - first - normed * second)


def silu_slope(values):
    sig = sigmoid(values)
    return sig * (1.0 + values * (1.0 - sig))


def kernel(
    ctx_count, data_count, head_count, level_count, scale_table,
    len_ref, table_ref, stamps_hbm, x_hbm, wp_hbm, wo_hbm, go_hbm,
    layer_hbm, grad_hbm, gt_ref,
    stamps_ref, xv, wp, wo, go, normed_ref, pre_ref, gate_ref, kv_all, st_all, scol, steps,
    q_all, g_all, qs, gs, buckets, sc, wt, mix, dq, own, tab1, tab2, tacc, layer_v, grad_v,
    load_sem, out_sem, st_send, st_recv, kv_send, kv_recv, q_send, q_recv, g_send, g_recv,
    t1_send, t1_recv, t2_send, t2_recv,
):
    rows, model_dim = xv.shape
    att = wo.shape[0]
    head_dim = att // head_count
    per = LANES // head_dim
    groups = att // LANES
    score_scale = head_dim ** (-0.5)
    me = lax.axis_index("ctx")
    my_dp = lax.axis_index("dp")
    ctx_at = lambda rank: {"ctx": rank}
    dp_at = lambda rank: {"dp": rank}

    def remote(src, dst, send_sem, recv_sem, where):
        return pltpu.make_async_remote_copy(
            src_ref=src, dst_ref=dst, send_sem=send_sem, recv_sem=recv_sem,
            device_id=where, device_id_type=MESH,
        )

    def loop(low, high, body):
        def step(index, carry):
            body(index)
            return carry

        lax.fori_loop(low, high, step, 0)

    load_x = pltpu.make_async_copy(x_hbm, xv, load_sem.at[0])
    load_kv = pltpu.make_async_copy(
        wp_hbm.at[:, pl.ds(2 * att, 2 * att)], wp.at[:, pl.ds(2 * att, 2 * att)], load_sem.at[1]
    )
    load_uq = pltpu.make_async_copy(
        wp_hbm.at[:, pl.ds(0, 2 * att)], wp.at[:, pl.ds(0, 2 * att)], load_sem.at[2]
    )
    load_go = pltpu.make_async_copy(go_hbm, go, load_sem.at[3])
    load_wo = pltpu.make_async_copy(wo_hbm, wo, load_sem.at[4])
    load_st = pltpu.make_async_copy(stamps_hbm, stamps_ref, load_sem.at[5])
    for load in (load_st, load_x, load_kv, load_uq, load_go, load_wo):
        load.start()

    barrier = pltpu.get_barrier_semaphore()
    ctx_peer = lambda offset: lax.rem(me + offset, ctx_count)
    dp_peer = lambda offset: lax.rem(my_dp + offset, data_count)

    @functools.partial(loop, 1, ctx_count)
    def _(offset):
        pl.semaphore_signal(
            barrier, inc=1, device_id=ctx_at(ctx_peer(offset)), device_id_type=MESH
        )

    @functools.partial(loop, 1, data_count)
    def _(offset):
        pl.semaphore_signal(
            barrier, inc=1, device_id=dp_at(dp_peer(offset)), device_id_type=MESH
        )

    length = len_ref[0]
    for head in range(head_count):
        running = table_ref[head, 0]
        steps[0, head] = running
        for level in range(level_count - 1):
            running = running + (table_ref[head, level + 1] - table_ref[head, level])
            steps[level + 1, head] = running

    load_st.wait()
    stamp_row = stamps_ref[...]
    st_all[me] = jnp.broadcast_to(stamp_row, (8, LANES))
    scol[...] = jnp.broadcast_to(stamp_row, (rows, LANES)).T

    load_x.wait()
    normed, inverse = norm_rows(xv[...].astype(F32))
    normed_ref[...] = normed
    rounded = normed.astype(BF16)
    load_kv.wait()
    pre_kv = mul(rounded, wp[:, 2 * att :])
    pre_ref[:, 2 * att :] = pre_kv
    kv_all[me] = (pre_kv * sigmoid(pre_kv)).astype(BF16)

    pl.semaphore_wait(barrier, ctx_count - 1 + data_count - 1)

    @functools.partial(loop, 1, ctx_count)
    def _(offset):
        rank = ctx_peer(offset)
        remote(
            st_all.at[me], st_all.at[me], st_send.at[rank], st_recv.at[me], ctx_at(rank)
        ).start()

    @functools.partial(loop, me + 1, ctx_count)
    def _(rank):
        remote(
            kv_all.at[me], kv_all.at[me], kv_send.at[rank], kv_recv.at[me], ctx_at(rank)
        ).start()

    lane = lax.broadcasted_iota(jnp.int32, (rows, LANES), 1)
    part = lane // head_dim

    def stack(values, target, slot):
        for group in range(groups):
            block = values[:, group * LANES : (group + 1) * LANES]
            for index in range(per):
                target[slot, group, index * rows : (index + 1) * rows, :] = jnp.where(
                    part == index, block, 0.0
                ).astype(BF16)

    def unstack(source):
        columns = []
        for group in range(groups):
            block = source[group, :rows, :]
            for index in range(1, per):
                block = jnp.where(
                    part == index, source[group, index * rows : (index + 1) * rows, :], block
                )
            columns.append(block)
        return jnp.concatenate(columns, axis=1)

    load_uq.wait()
    pre_uq = mul(rounded, wp[:, : 2 * att])
    pre_ref[:, : 2 * att] = pre_uq
    act_uq = pre_uq * sigmoid(pre_uq)
    gate_ref[...] = act_uq[:, :att].astype(BF16).astype(F32)
    own_q = act_uq[:, att:] * score_scale
    q_all[me] = own_q.astype(BF16)

    @functools.partial(loop, 0, me)
    def _(rank):
        remote(
            q_all.at[me], q_all.at[me], q_send.at[rank], q_recv.at[me], ctx_at(rank)
        ).start()

    stack(own_q, qs, me)
    load_go.wait()
    load_wo.wait()
    grad_gated = mul(go[...], wo[...], NT)

    chunk = 32

    def add_bias(block, columns, key_stamps):
        for first in range(0, rows, chunk):
            gap = columns[first : first + chunk, :] - key_stamps
            bucket = jnp.zeros(gap.shape, jnp.int32)
            bias = [jnp.full(gap.shape, steps[0, head], F32) for head in range(head_count)]
            for level in range(level_count - 1):
                above = gap >= (1 << level)
                bucket = jnp.where(above, level + 1, bucket)
                bias = [
                    jnp.where(above, steps[level + 1, head], bias[head])
                    for head in range(head_count)
                ]
            buckets[block, first : first + chunk, :] = bucket
            for head in range(head_count):
                start = (head % per) * rows + first
                sc[block, head // per, start : start + chunk, :] = bias[head]

    def wait_stamps(rank):
        remote(
            st_all.at[rank], st_all.at[rank], st_send.at[rank], st_recv.at[rank], ctx_at(rank)
        ).wait_recv()

    @functools.partial(loop, 0, me + 1)
    def _(turn):
        block = me - turn

        @pl.when(turn > 0)
        def _():
            wait_stamps(block)

        add_bias(block, scol[...], st_all[block][0:1, :])

    def score_block(block, query_at, first_query, first_key, keys_at):
        query_pos = first_query * rows + lax.broadcasted_iota(jnp.int32, (rows, LANES), 0)
        share = 1.0 / (jnp.minimum(query_pos, length - 1) + 1).astype(F32)
        key_pos = first_key * rows + lane
        part_share = jnp.where((key_pos <= query_pos) & (key_pos < length), share, 0.0)
        shares = jnp.concatenate([part_share] * per, axis=0)
        for group in range(groups):
            keys = kv_all[keys_at, :, group * LANES : (group + 1) * LANES]
            scores = mul(qs[query_at, group], keys, NT) + sc[block, group]
            sig = sigmoid(scores)
            shared = sig * shares
            sc[block, group] = shared * (1.0 + scores * (1.0 - sig))
            wt[block, group] = (scores * shared).astype(BF16)

    mix[...] = jnp.zeros_like(mix)
    dq[...] = jnp.zeros_like(dq)

    @functools.partial(loop, 0, me + 1)
    def _(turn):
        block = me - turn

        @pl.when(turn > 0)
        def _():
            remote(
                kv_all.at[block], kv_all.at[block], kv_send.at[block], kv_recv.at[block],
                ctx_at(block),
            ).wait_recv()

        score_block(block, me, me, block, block)
        for group in range(groups):
            values = kv_all[block, :, att + group * LANES : att + (group + 1) * LANES]
            mix[group] += mul(wt[block, group], values)

    mixed_norm, mixed_inv = norm_rows(unstack(mix))
    gate = gate_ref[...]
    grad_units = grad_gated * mixed_norm
    own_g = norm_back(grad_gated * gate, mixed_norm, mixed_inv)
    g_all[me] = own_g.astype(BF16)

    @functools.partial(loop, 0, me)
    def _(rank):
        remote(
            g_all.at[me], g_all.at[me], g_send.at[rank], g_recv.at[me], ctx_at(rank)
        ).start()

    stack(own_g, gs, me)

    @functools.partial(loop, me + 1, ctx_count)
    def _(block):
        wait_stamps(block)
        stamp_block = jnp.broadcast_to(st_all[block][0:1, :], (rows, LANES))
        add_bias(block, stamp_block.T, st_all[me][0:1, :])
        remote(
            q_all.at[block], q_all.at[block], q_send.at[block], q_recv.at[block], ctx_at(block)
        ).wait_recv()
        stack(q_all[block].astype(F32), qs, block)
        score_block(block, block, block, me, me)

    def back_scores(block, query_at, keys_at, group):
        values = kv_all[keys_at, :, att + group * LANES : att + (group + 1) * LANES]
        return (mul(gs[query_at, group], values, NT) * sc[block, group]).astype(BF16)

    def add_key_grads(block, group, grad_scores):
        low, high = group * LANES, (group + 1) * LANES
        own[:, low:high] += mul(grad_scores, qs[block, group], TN)
        own[:, att + low : att + high] += mul(wt[block, group], gs[block, group], TN)

    own[...] = jnp.zeros_like(own)

    @functools.partial(loop, 0, me + 1)
    def _(block):
        for group in range(groups):
            keys = kv_all[block, :, group * LANES : (group + 1) * LANES]
            grad_scores = back_scores(block, me, block, group)
            sc[block, group] = grad_scores.astype(F32)
            dq[group] += mul(grad_scores, keys)

            @pl.when(block == me)
            def _():
                add_key_grads(block, group, grad_scores)

    tacc[...] = jnp.zeros_like(tacc)

    @functools.partial(loop, 0, me + 1)
    def _(block):
        bucket = buckets[block]
        for level in range(level_count):
            found = bucket == level
            for head in range(head_count):
                start = (head % per) * rows
                terms = jnp.where(found, sc[block, head // per, start : start + rows, :], 0.0)
                tacc[head, level] += jnp.sum(terms.reshape(rows // 8, 8, LANES), axis=0)

    cells = head_count * level_count
    summed = jnp.concatenate(
        [
            jnp.sum(tacc[...], axis=2).reshape(cells, LANES),
            jnp.zeros((LANES - cells, LANES), F32),
        ],
        axis=0,
    )
    local = jnp.broadcast_to(jnp.sum(summed.T, axis=0, keepdims=True), (8, LANES))
    tab1[me] = local

    @functools.partial(loop, 1, ctx_count)
    def _(offset):
        rank = ctx_peer(offset)
        remote(
            tab1.at[me], tab1.at[me], t1_send.at[rank], t1_recv.at[me], ctx_at(rank)
        ).start()

    gated = (mixed_norm * gate).astype(BF16)
    layer_v[...] = (xv[...].astype(F32) + mul(gated, wo[...])).astype(BF16)
    write_layer = pltpu.make_async_copy(layer_v, layer_hbm, out_sem.at[0])
    write_layer.start()

    slope_uq = silu_slope(pre_ref[:, : 2 * att])
    grad_uq = jnp.concatenate([grad_units, unstack(dq) * score_scale], axis=1) * slope_uq
    grad_normed = mul(grad_uq.astype(BF16), wp[:, : 2 * att], NT)

    @functools.partial(loop, me + 1, ctx_count)
    def _(rank):
        remote(
            g_all.at[rank], g_all.at[rank], g_send.at[rank], g_recv.at[rank], ctx_at(rank)
        ).wait_recv()
        stack(g_all[rank].astype(F32), gs, rank)
        for group in range(groups):
            add_key_grads(rank, group, back_scores(rank, rank, me, group))

    @functools.partial(loop, 1, ctx_count)
    def _(offset):
        rank = ctx_peer(offset)
        remote(
            tab1.at[rank], tab1.at[rank], t1_send.at[rank], t1_recv.at[rank], ctx_at(rank)
        ).wait_recv()

    group_sum = tab1[0]
    for rank in range(1, ctx_count):
        group_sum = group_sum + tab1[rank]
    tab2[my_dp] = group_sum

    @functools.partial(loop, 1, data_count)
    def _(offset):
        rank = dp_peer(offset)
        remote(
            tab2.at[my_dp], tab2.at[my_dp], t2_send.at[rank], t2_recv.at[my_dp], dp_at(rank)
        ).start()

    grad_kv = own[...] * silu_slope(pre_ref[:, 2 * att :])
    grad_normed = grad_normed + mul(grad_kv.astype(BF16), wp[:, 2 * att :], NT)
    grad_v[...] = (
        norm_back(grad_normed, normed_ref[...], inverse) + go[...].astype(F32)
    ).astype(BF16)
    write_grad = pltpu.make_async_copy(grad_v, grad_hbm, out_sem.at[1])
    write_grad.start()

    @functools.partial(loop, 1, data_count)
    def _(offset):
        rank = dp_peer(offset)
        remote(
            tab2.at[rank], tab2.at[rank], t2_send.at[rank], t2_recv.at[rank], dp_at(rank)
        ).wait_recv()

    total = tab2[0]
    for rank in range(1, data_count):
        total = total + tab2[rank]
    for head in range(head_count):
        cells = total[0:1, head * level_count : (head + 1) * level_count]
        gt_ref[head : head + 1, :] = cells * scale_table

    @functools.partial(loop, me + 1, ctx_count)
    def _(rank):
        remote(
            kv_all.at[me], kv_all.at[me], kv_send.at[rank], kv_recv.at[me], ctx_at(rank)
        ).wait_send()

    @functools.partial(loop, 0, me)
    def _(block):
        remote(
            q_all.at[me], q_all.at[me], q_send.at[block], q_recv.at[me], ctx_at(block)
        ).wait_send()
        remote(
            g_all.at[me], g_all.at[me], g_send.at[block], g_recv.at[me], ctx_at(block)
        ).wait_send()

    @functools.partial(loop, 1, ctx_count)
    def _(offset):
        rank = ctx_peer(offset)
        remote(
            tab1.at[me], tab1.at[me], t1_send.at[rank], t1_recv.at[me], ctx_at(rank)
        ).wait_send()
        remote(
            st_all.at[me], st_all.at[me], st_send.at[rank], st_recv.at[me], ctx_at(rank)
        ).wait_send()

    @functools.partial(loop, 1, data_count)
    def _(offset):
        rank = dp_peer(offset)
        remote(
            tab2.at[my_dp], tab2.at[my_dp], t2_send.at[rank], t2_recv.at[my_dp], dp_at(rank)
        ).wait_send()

    write_layer.wait()
    write_grad.wait()


def hand_over(*refs):
    count = len(refs) // 2
    sems = refs[-1]
    copies = []
    for index in range(count):
        source, target = refs[index], refs[count + index]
        size = min(32, source.shape[0])
        for first in range(0, source.shape[0], size):
            part = pl.ds(first, size)
            copies.append(
                pltpu.make_async_copy(source.at[part], target.at[part], sems.at[len(copies)])
            )
    for copy in copies:
        copy.start()
    for copy in copies:
        copy.wait()


def on_device(actions, stamps, lengths, w_proj, w_out, bias_table, grad_out):
    rows = actions.shape[1]
    model_dim = actions.shape[2]
    level_count, head_count = bias_table.shape
    att = w_out.shape[0]
    ctx_count = lax.axis_size("ctx")
    data_count = lax.axis_size("dp")
    groups = att // LANES
    per = LANES // (att // head_count)
    scale_table = 1.0 / math.sqrt(rows * ctx_count * data_count)
    vmem = pl.BlockSpec(memory_space=pltpu.VMEM)
    smem = pl.BlockSpec(memory_space=pltpu.SMEM)
    anywhere = pl.BlockSpec(memory_space=pltpu.HBM)
    dma = pltpu.SemaphoreType.DMA
    layer_rows, grad_rows, grad_table = pl.pallas_call(
        functools.partial(kernel, ctx_count, data_count, head_count, level_count, scale_table),
        out_shape=(
            jax.ShapeDtypeStruct((rows, model_dim), BF16),
            jax.ShapeDtypeStruct((rows, model_dim), BF16),
            jax.ShapeDtypeStruct((head_count, level_count), F32),
        ),
        in_specs=[smem, smem, anywhere, anywhere, anywhere, anywhere, anywhere],
        out_specs=(anywhere, anywhere, vmem),
        scratch_shapes=[
            pltpu.VMEM((1, rows), jnp.int32),
            pltpu.VMEM((rows, model_dim), BF16),
            pltpu.VMEM((model_dim, 4 * att), BF16),
            pltpu.VMEM((att, model_dim), BF16),
            pltpu.VMEM((rows, model_dim), BF16),
            pltpu.VMEM((rows, model_dim), F32),
            pltpu.VMEM((rows, 4 * att), F32),
            pltpu.VMEM((rows, att), F32),
            pltpu.VMEM((ctx_count, rows, 2 * att), BF16),
            pltpu.VMEM((ctx_count, 8, LANES), jnp.int32),
            pltpu.VMEM((rows, LANES), jnp.int32),
            pltpu.SMEM((level_count, head_count), F32),
            pltpu.VMEM((ctx_count, rows, att), BF16),
            pltpu.VMEM((ctx_count, rows, att), BF16),
            pltpu.VMEM((ctx_count, groups, per * rows, LANES), BF16),
            pltpu.VMEM((ctx_count, groups, per * rows, LANES), BF16),
            pltpu.VMEM((ctx_count, rows, LANES), jnp.int32),
            pltpu.VMEM((ctx_count, groups, per * rows, LANES), F32),
            pltpu.VMEM((ctx_count, groups, per * rows, LANES), BF16),
            pltpu.VMEM((groups, per * rows, LANES), F32),
            pltpu.VMEM((groups, per * rows, LANES), F32),
            pltpu.VMEM((rows, 2 * att), F32),
            pltpu.VMEM((ctx_count, 8, LANES), F32),
            pltpu.VMEM((data_count, 8, LANES), F32),
            pltpu.VMEM((head_count, level_count, 8, LANES), F32),
            pltpu.VMEM((rows, model_dim), BF16),
            pltpu.VMEM((rows, model_dim), BF16),
            dma((6,)),
            dma((2,)),
            dma((ctx_count,)),
            dma((ctx_count,)),
            dma((ctx_count,)),
            dma((ctx_count,)),
            dma((ctx_count,)),
            dma((ctx_count,)),
            dma((ctx_count,)),
            dma((ctx_count,)),
            dma((ctx_count,)),
            dma((ctx_count,)),
            dma((data_count,)),
            dma((data_count,)),
        ],
        compiler_params=pltpu.CompilerParams(
            collective_id=0, has_side_effects=True, vmem_limit_bytes=60 * 1024 * 1024
        ),
    )(
        lengths,
        bias_table.T,
        stamps,
        actions.reshape(rows, model_dim),
        w_proj,
        w_out,
        grad_out.reshape(rows, model_dim),
    )
    results = (layer_rows, grad_rows, grad_table)
    layer_rows, grad_rows, grad_table = pl.pallas_call(
        hand_over,
        out_shape=tuple(jax.ShapeDtypeStruct(one.shape, one.dtype) for one in results),
        in_specs=[anywhere] * 3,
        out_specs=(anywhere,) * 3,
        scratch_shapes=[dma((2 * (rows // 32) + 1,))],
        compiler_params=pltpu.CompilerParams(vmem_limit_bytes=60 * 1024 * 1024),
    )(*results)
    return (
        layer_rows.reshape(1, rows, model_dim),
        grad_rows.reshape(1, rows, model_dim),
        grad_table.T,
    )


def solution(mesh):
    in_specs = (P("dp", "ctx", None), P("dp", "ctx"), P("dp"), P(), P(), P(), P("dp", "ctx", None))
    out_specs = (P("dp", "ctx", None), P("dp", "ctx", None), P())
    return jax.shard_map(
        on_device, mesh=mesh, in_specs=in_specs, out_specs=out_specs, check_vma=False
    )
```

```python
import functools
import math

import jax
import jax.numpy as jnp
from jax import lax
from jax.experimental import pallas as pl
from jax.experimental.pallas import tpu as pltpu
from jax.sharding import PartitionSpec as P

EPS = 1e-05
MESH = pl.DeviceIdType.MESH
LANES = 128
F32 = jnp.float32
BF16 = jnp.bfloat16
NT = (((1,), (1,)), ((), ()))
TN = (((0,), (0,)), ((), ()))
NN = (((1,), (0,)), ((), ()))


def mul(left, right, dims=NN):
    return lax.dot_general(left, right, dims, preferred_element_type=F32)


def sigmoid(values):
    return 0.5 * jnp.tanh(0.5 * values) + 0.5


def norm_rows(values):
    row_mean = jnp.mean(values, axis=-1, keepdims=True)
    centred = values - row_mean
    spread = jnp.mean(centred * centred, axis=-1, keepdims=True)
    inverse = lax.rsqrt(spread + EPS)
    return centred * inverse, inverse


def norm_back(incoming, normed, inverse):
    first = jnp.mean(incoming, axis=-1, keepdims=True)
    second = jnp.mean(incoming * normed, axis=-1, keepdims=True)
    return inverse * (incoming - first - normed * second)


def silu_slope(values):
    sig = sigmoid(values)
    return sig * (1.0 + values * (1.0 - sig))


def kernel(
    ctx_count, data_count, head_count, level_count, scale_table,
    len_ref, table_ref, stamps_hbm, x_hbm, wp_hbm, wo_hbm, go_hbm,
    layer_hbm, grad_hbm, gt_ref,
    stamps_ref, xv, wp, wo, go, normed_ref, pre_ref, gate_ref, kv_all, st_all, scol, steps,
    q_all, g_all, qs, gs, buckets, sc, wt, mix, dq, own, tab1, tab2, tacc, layer_v, grad_v,
    load_sem, out_sem, st_send, st_recv, kv_send, kv_recv, q_send, q_recv, g_send, g_recv,
    t1_send, t1_recv, t2_send, t2_recv,
):
    rows, model_dim = xv.shape
    att = wo.shape[0]
    head_dim = att // head_count
    per = LANES // head_dim
    groups = att // LANES
    score_scale = head_dim ** (-0.5)
    me = lax.axis_index("ctx")
    my_dp = lax.axis_index("dp")
    ctx_at = lambda rank: {"ctx": rank}
    dp_at = lambda rank: {"dp": rank}

    def remote(src, dst, send_sem, recv_sem, where):
        return pltpu.make_async_remote_copy(
            src_ref=src, dst_ref=dst, send_sem=send_sem, recv_sem=recv_sem,
            device_id=where, device_id_type=MESH,
        )

    def loop(low, high, body):
        def step(index, carry):
            body(index)
            return carry

        lax.fori_loop(low, high, step, 0)

    load_x = pltpu.make_async_copy(x_hbm, xv, load_sem.at[0])
    load_kv = pltpu.make_async_copy(
        wp_hbm.at[:, pl.ds(2 * att, 2 * att)], wp.at[:, pl.ds(2 * att, 2 * att)], load_sem.at[1]
    )
    load_uq = pltpu.make_async_copy(
        wp_hbm.at[:, pl.ds(0, 2 * att)], wp.at[:, pl.ds(0, 2 * att)], load_sem.at[2]
    )
    load_go = pltpu.make_async_copy(go_hbm, go, load_sem.at[3])
    load_wo = pltpu.make_async_copy(wo_hbm, wo, load_sem.at[4])
    load_st = pltpu.make_async_copy(stamps_hbm, stamps_ref, load_sem.at[5])
    for load in (load_st, load_x, load_kv, load_uq, load_go, load_wo):
        load.start()

    barrier = pltpu.get_barrier_semaphore()
    ctx_peer = lambda offset: lax.rem(me + offset, ctx_count)
    dp_peer = lambda offset: lax.rem(my_dp + offset, data_count)

    @functools.partial(loop, 1, ctx_count)
    def _(offset):
        pl.semaphore_signal(
            barrier, inc=1, device_id=ctx_at(ctx_peer(offset)), device_id_type=MESH
        )

    @functools.partial(loop, 1, data_count)
    def _(offset):
        pl.semaphore_signal(
            barrier, inc=1, device_id=dp_at(dp_peer(offset)), device_id_type=MESH
        )

    length = len_ref[0]
    for head in range(head_count):
        running = table_ref[head, 0]
        steps[0, head] = running
        for level in range(level_count - 1):
            running = running + (table_ref[head, level + 1] - table_ref[head, level])
            steps[level + 1, head] = running

    load_st.wait()
    stamp_row = stamps_ref[...]
    st_all[me] = jnp.broadcast_to(stamp_row, (8, LANES))
    scol[...] = jnp.broadcast_to(stamp_row, (rows, LANES)).T

    load_x.wait()
    normed, inverse = norm_rows(xv[...].astype(F32))
    normed_ref[...] = normed
    rounded = normed.astype(BF16)
    load_kv.wait()
    pre_kv = mul(rounded, wp[:, 2 * att :])
    pre_ref[:, 2 * att :] = pre_kv
    kv_all[me] = (pre_kv * sigmoid(pre_kv)).astype(BF16)

    pl.semaphore_wait(barrier, ctx_count - 1 + data_count - 1)

    @functools.partial(loop, 1, ctx_count)
    def _(offset):
        rank = ctx_peer(offset)
        remote(
            st_all.at[me], st_all.at[me], st_send.at[rank], st_recv.at[me], ctx_at(rank)
        ).start()

    @functools.partial(loop, me + 1, ctx_count)
    def _(rank):
        remote(
            kv_all.at[me], kv_all.at[me], kv_send.at[rank], kv_recv.at[me], ctx_at(rank)
        ).start()

    lane = lax.broadcasted_iota(jnp.int32, (rows, LANES), 1)
    part = lane // head_dim

    def stack(values, target, slot):
        for group in range(groups):
            block = values[:, group * LANES : (group + 1) * LANES]
            for index in range(per):
                target[slot, group, index * rows : (index + 1) * rows, :] = jnp.where(
                    part == index, block, 0.0
                ).astype(BF16)

    def unstack(source):
        columns = []
        for group in range(groups):
            block = source[group, :rows, :]
            for index in range(1, per):
                block = jnp.where(
                    part == index, source[group, index * rows : (index + 1) * rows, :], block
                )
            columns.append(block)
        return jnp.concatenate(columns, axis=1)

    load_uq.wait()
    pre_uq = mul(rounded, wp[:, : 2 * att])
    pre_ref[:, : 2 * att] = pre_uq
    act_uq = pre_uq * sigmoid(pre_uq)
    gate_ref[...] = act_uq[:, :att].astype(BF16).astype(F32)
    own_q = act_uq[:, att:] * score_scale
    q_all[me] = own_q.astype(BF16)

    @functools.partial(loop, 0, me)
    def _(rank):
        remote(
            q_all.at[me], q_all.at[me], q_send.at[rank], q_recv.at[me], ctx_at(rank)
        ).start()

    stack(own_q, qs, me)
    load_go.wait()
    load_wo.wait()
    grad_gated = mul(go[...], wo[...], NT)

    chunk = 32

    def add_bias(block, columns, key_stamps):
        for first in range(0, rows, chunk):
            gap = columns[first : first + chunk, :] - key_stamps
            bucket = jnp.zeros(gap.shape, jnp.int32)
            bias = [jnp.full(gap.shape, steps[0, head], F32) for head in range(head_count)]
            for level in range(level_count - 1):
                above = gap >= (1 << level)
                bucket = jnp.where(above, level + 1, bucket)
                bias = [
                    jnp.where(above, steps[level + 1, head], bias[head])
                    for head in range(head_count)
                ]
            buckets[block, first : first + chunk, :] = bucket
            for head in range(head_count):
                start = (head % per) * rows + first
                sc[block, head // per, start : start + chunk, :] = bias[head]

    def wait_stamps(rank):
        remote(
            st_all.at[rank], st_all.at[rank], st_send.at[rank], st_recv.at[rank], ctx_at(rank)
        ).wait_recv()

    @functools.partial(loop, 0, me + 1)
    def _(turn):
        block = me - turn

        @pl.when(turn > 0)
        def _():
            wait_stamps(block)

        add_bias(block, scol[...], st_all[block][0:1, :])

    def score_block(block, query_at, first_query, first_key, keys_at):
        query_pos = first_query * rows + lax.broadcasted_iota(jnp.int32, (rows, LANES), 0)
        share = 1.0 / (jnp.minimum(query_pos, length - 1) + 1).astype(F32)
        key_pos = first_key * rows + lane
        part_share = jnp.where((key_pos <= query_pos) & (key_pos < length), share, 0.0)
        shares = jnp.concatenate([part_share] * per, axis=0)
        for group in range(groups):
            keys = kv_all[keys_at, :, group * LANES : (group + 1) * LANES]
            scores = mul(qs[query_at, group], keys, NT) + sc[block, group]
            sig = sigmoid(scores)
            shared = sig * shares
            sc[block, group] = shared * (1.0 + scores * (1.0 - sig))
            wt[block, group] = (scores * shared).astype(BF16)

    mix[...] = jnp.zeros_like(mix)
    dq[...] = jnp.zeros_like(dq)

    @functools.partial(loop, 0, me + 1)
    def _(turn):
        block = me - turn

        @pl.when(turn > 0)
        def _():
            remote(
                kv_all.at[block], kv_all.at[block], kv_send.at[block], kv_recv.at[block],
                ctx_at(block),
            ).wait_recv()

        score_block(block, me, me, block, block)
        for group in range(groups):
            values = kv_all[block, :, att + group * LANES : att + (group + 1) * LANES]
            mix[group] += mul(wt[block, group], values)

    mixed_norm, mixed_inv = norm_rows(unstack(mix))
    gate = gate_ref[...]
    grad_units = grad_gated * mixed_norm
    own_g = norm_back(grad_gated * gate, mixed_norm, mixed_inv)
    g_all[me] = own_g.astype(BF16)

    @functools.partial(loop, 0, me)
    def _(rank):
        remote(
            g_all.at[me], g_all.at[me], g_send.at[rank], g_recv.at[me], ctx_at(rank)
        ).start()

    stack(own_g, gs, me)

    @functools.partial(loop, me + 1, ctx_count)
    def _(block):
        wait_stamps(block)
        stamp_block = jnp.broadcast_to(st_all[block][0:1, :], (rows, LANES))
        add_bias(block, stamp_block.T, st_all[me][0:1, :])
        remote(
            q_all.at[block], q_all.at[block], q_send.at[block], q_recv.at[block], ctx_at(block)
        ).wait_recv()
        stack(q_all[block].astype(F32), qs, block)
        score_block(block, block, block, me, me)

    def back_scores(block, query_at, keys_at, group):
        values = kv_all[keys_at, :, att + group * LANES : att + (group + 1) * LANES]
        return (mul(gs[query_at, group], values, NT) * sc[block, group]).astype(BF16)

    def add_key_grads(block, group, grad_scores):
        low, high = group * LANES, (group + 1) * LANES
        own[:, low:high] += mul(grad_scores, qs[block, group], TN)
        own[:, att + low : att + high] += mul(wt[block, group], gs[block, group], TN)

    own[...] = jnp.zeros_like(own)

    @functools.partial(loop, 0, me + 1)
    def _(block):
        for group in range(groups):
            keys = kv_all[block, :, group * LANES : (group + 1) * LANES]
            grad_scores = back_scores(block, me, block, group)
            sc[block, group] = grad_scores.astype(F32)
            dq[group] += mul(grad_scores, keys)

            @pl.when(block == me)
            def _():
                add_key_grads(block, group, grad_scores)

    tacc[...] = jnp.zeros_like(tacc)

    @functools.partial(loop, 0, me + 1)
    def _(block):
        bucket = buckets[block]
        for level in range(level_count):
            found = bucket == level
            for head in range(head_count):
                start = (head % per) * rows
                terms = jnp.where(found, sc[block, head // per, start : start + rows, :], 0.0)
                tacc[head, level] += jnp.sum(terms.reshape(rows // 8, 8, LANES), axis=0)

    cells = head_count * level_count
    summed = jnp.concatenate(
        [
            jnp.sum(tacc[...], axis=2).reshape(cells, LANES),
            jnp.zeros((LANES - cells, LANES), F32),
        ],
        axis=0,
    )
    local = jnp.broadcast_to(jnp.sum(summed.T, axis=0, keepdims=True), (8, LANES))
    tab1[me] = local

    @functools.partial(loop, 1, ctx_count)
    def _(offset):
        rank = ctx_peer(offset)
        remote(
            tab1.at[me], tab1.at[me], t1_send.at[rank], t1_recv.at[me], ctx_at(rank)
        ).start()

    gated = (mixed_norm * gate).astype(BF16)
    layer_v[...] = (xv[...].astype(F32) + mul(gated, wo[...])).astype(BF16)
    write_layer = pltpu.make_async_copy(layer_v, layer_hbm, out_sem.at[0])
    write_layer.start()

    slope_uq = silu_slope(pre_ref[:, : 2 * att])
    grad_uq = jnp.concatenate([grad_units, unstack(dq) * score_scale], axis=1) * slope_uq
    grad_normed = mul(grad_uq.astype(BF16), wp[:, : 2 * att], NT)

    @functools.partial(loop, me + 1, ctx_count)
    def _(rank):
        remote(
            g_all.at[rank], g_all.at[rank], g_send.at[rank], g_recv.at[rank], ctx_at(rank)
        ).wait_recv()
        stack(g_all[rank].astype(F32), gs, rank)
        for group in range(groups):
            add_key_grads(rank, group, back_scores(rank, rank, me, group))

    @functools.partial(loop, 1, ctx_count)
    def _(offset):
        rank = ctx_peer(offset)
        remote(
            tab1.at[rank], tab1.at[rank], t1_send.at[rank], t1_recv.at[rank], ctx_at(rank)
        ).wait_recv()

    group_sum = tab1[0]
    for rank in range(1, ctx_count):
        group_sum = group_sum + tab1[rank]
    tab2[my_dp] = group_sum

    @functools.partial(loop, 1, data_count)
    def _(offset):
        rank = dp_peer(offset)
        remote(
            tab2.at[my_dp], tab2.at[my_dp], t2_send.at[rank], t2_recv.at[my_dp], dp_at(rank)
        ).start()

    grad_kv = own[...] * silu_slope(pre_ref[:, 2 * att :])
    grad_normed = grad_normed + mul(grad_kv.astype(BF16), wp[:, 2 * att :], NT)
    grad_v[...] = (
        norm_back(grad_normed, normed_ref[...], inverse) + go[...].astype(F32)
    ).astype(BF16)
    write_grad = pltpu.make_async_copy(grad_v, grad_hbm, out_sem.at[1])
    write_grad.start()

    @functools.partial(loop, 1, data_count)
    def _(offset):
        rank = dp_peer(offset)
        remote(
            tab2.at[rank], tab2.at[rank], t2_send.at[rank], t2_recv.at[rank], dp_at(rank)
        ).wait_recv()

    total = tab2[0]
    for rank in range(1, data_count):
        total = total + tab2[rank]
    for head in range(head_count):
        cells = total[0:1, head * level_count : (head + 1) * level_count]
        gt_ref[head : head + 1, :] = cells * scale_table

    @functools.partial(loop, me + 1, ctx_count)
    def _(rank):
        remote(
            kv_all.at[me], kv_all.at[me], kv_send.at[rank], kv_recv.at[me], ctx_at(rank)
        ).wait_send()

    @functools.partial(loop, 0, me)
    def _(block):
        remote(
            q_all.at[me], q_all.at[me], q_send.at[block], q_recv.at[me], ctx_at(block)
        ).wait_send()
        remote(
            g_all.at[me], g_all.at[me], g_send.at[block], g_recv.at[me], ctx_at(block)
        ).wait_send()

    @functools.partial(loop, 1, ctx_count)
    def _(offset):
        rank = ctx_peer(offset)
        remote(
            tab1.at[me], tab1.at[me], t1_send.at[rank], t1_recv.at[me], ctx_at(rank)
        ).wait_send()
        remote(
            st_all.at[me], st_all.at[me], st_send.at[rank], st_recv.at[me], ctx_at(rank)
        ).wait_send()

    @functools.partial(loop, 1, data_count)
    def _(offset):
        rank = dp_peer(offset)
        remote(
            tab2.at[my_dp], tab2.at[my_dp], t2_send.at[rank], t2_recv.at[my_dp], dp_at(rank)
        ).wait_send()

    write_layer.wait()
    write_grad.wait()


def hand_over(*refs):
    sources, targets, held = refs[:3], refs[3:6], refs[6:9]
    in_sems, out_sems = refs[9:]
    loads, stores = [], []
    for source, target, buffer in zip(sources, targets, held):
        size = min(64, source.shape[0])
        for first in range(0, source.shape[0], size):
            part, index = pl.ds(first, size), len(loads)
            loads.append(
                pltpu.make_async_copy(source.at[part], buffer.at[part], in_sems.at[index])
            )
            stores.append(
                pltpu.make_async_copy(buffer.at[part], target.at[part], out_sems.at[index])
            )
    for load in loads:
        load.start()
    for load, store in zip(loads, stores):
        load.wait()
        store.start()
    for store in stores:
        store.wait()


def on_device(actions, stamps, lengths, w_proj, w_out, bias_table, grad_out):
    rows = actions.shape[1]
    model_dim = actions.shape[2]
    level_count, head_count = bias_table.shape
    att = w_out.shape[0]
    ctx_count = lax.axis_size("ctx")
    data_count = lax.axis_size("dp")
    groups = att // LANES
    per = LANES // (att // head_count)
    scale_table = 1.0 / math.sqrt(rows * ctx_count * data_count)
    vmem = pl.BlockSpec(memory_space=pltpu.VMEM)
    smem = pl.BlockSpec(memory_space=pltpu.SMEM)
    anywhere = pl.BlockSpec(memory_space=pltpu.HBM)
    dma = pltpu.SemaphoreType.DMA
    layer_rows, grad_rows, grad_table = pl.pallas_call(
        functools.partial(kernel, ctx_count, data_count, head_count, level_count, scale_table),
        out_shape=(
            jax.ShapeDtypeStruct((rows, model_dim), BF16),
            jax.ShapeDtypeStruct((rows, model_dim), BF16),
            jax.ShapeDtypeStruct((head_count, level_count), F32),
        ),
        in_specs=[smem, smem, anywhere, anywhere, anywhere, anywhere, anywhere],
        out_specs=(anywhere, anywhere, vmem),
        scratch_shapes=[
            pltpu.VMEM((1, rows), jnp.int32),
            pltpu.VMEM((rows, model_dim), BF16),
            pltpu.VMEM((model_dim, 4 * att), BF16),
            pltpu.VMEM((att, model_dim), BF16),
            pltpu.VMEM((rows, model_dim), BF16),
            pltpu.VMEM((rows, model_dim), F32),
            pltpu.VMEM((rows, 4 * att), F32),
            pltpu.VMEM((rows, att), F32),
            pltpu.VMEM((ctx_count, rows, 2 * att), BF16),
            pltpu.VMEM((ctx_count, 8, LANES), jnp.int32),
            pltpu.VMEM((rows, LANES), jnp.int32),
            pltpu.SMEM((level_count, head_count), F32),
            pltpu.VMEM((ctx_count, rows, att), BF16),
            pltpu.VMEM((ctx_count, rows, att), BF16),
            pltpu.VMEM((ctx_count, groups, per * rows, LANES), BF16),
            pltpu.VMEM((ctx_count, groups, per * rows, LANES), BF16),
            pltpu.VMEM((ctx_count, rows, LANES), jnp.int32),
            pltpu.VMEM((ctx_count, groups, per * rows, LANES), F32),
            pltpu.VMEM((ctx_count, groups, per * rows, LANES), BF16),
            pltpu.VMEM((groups, per * rows, LANES), F32),
            pltpu.VMEM((groups, per * rows, LANES), F32),
            pltpu.VMEM((rows, 2 * att), F32),
            pltpu.VMEM((ctx_count, 8, LANES), F32),
            pltpu.VMEM((data_count, 8, LANES), F32),
            pltpu.VMEM((head_count, level_count, 8, LANES), F32),
            pltpu.VMEM((rows, model_dim), BF16),
            pltpu.VMEM((rows, model_dim), BF16),
            dma((6,)),
            dma((2,)),
            dma((ctx_count,)),
            dma((ctx_count,)),
            dma((ctx_count,)),
            dma((ctx_count,)),
            dma((ctx_count,)),
            dma((ctx_count,)),
            dma((ctx_count,)),
            dma((ctx_count,)),
            dma((ctx_count,)),
            dma((ctx_count,)),
            dma((data_count,)),
            dma((data_count,)),
        ],
        compiler_params=pltpu.CompilerParams(
            collective_id=0, has_side_effects=True, vmem_limit_bytes=60 * 1024 * 1024
        ),
    )(
        lengths,
        bias_table.T,
        stamps,
        actions.reshape(rows, model_dim),
        w_proj,
        w_out,
        grad_out.reshape(rows, model_dim),
    )
    results = (layer_rows, grad_rows, grad_table)
    layer_rows, grad_rows, grad_table = pl.pallas_call(
        hand_over,
        out_shape=tuple(jax.ShapeDtypeStruct(one.shape, one.dtype) for one in results),
        in_specs=[anywhere] * 3,
        out_specs=(anywhere,) * 3,
        scratch_shapes=[pltpu.VMEM(one.shape, one.dtype) for one in results]
        + [dma((2 * (rows // 64) + 1,))] * 2,
        compiler_params=pltpu.CompilerParams(vmem_limit_bytes=60 * 1024 * 1024),
    )(*results)
    return (
        layer_rows.reshape(1, rows, model_dim),
        grad_rows.reshape(1, rows, model_dim),
        grad_table.T,
    )


def solution(mesh):
    in_specs = (P("dp", "ctx", None), P("dp", "ctx"), P("dp"), P(), P(), P(), P("dp", "ctx", None))
    out_specs = (P("dp", "ctx", None), P("dp", "ctx", None), P())
    return jax.shard_map(
        on_device, mesh=mesh, in_specs=in_specs, out_specs=out_specs, check_vma=False
    )
```

```python
import functools
import math

import jax
import jax.numpy as jnp
from jax import lax
from jax.experimental import pallas as pl
from jax.experimental.pallas import tpu as pltpu
from jax.sharding import PartitionSpec as P

EPS = 1e-05
MESH = pl.DeviceIdType.MESH
LANES = 128
F32 = jnp.float32
BF16 = jnp.bfloat16
NT = (((1,), (1,)), ((), ()))
TN = (((0,), (0,)), ((), ()))
NN = (((1,), (0,)), ((), ()))


def mul(left, right, dims=NN):
    return lax.dot_general(left, right, dims, preferred_element_type=F32)


def sigmoid(values):
    return 0.5 * jnp.tanh(0.5 * values) + 0.5


def norm_rows(values):
    row_mean = jnp.mean(values, axis=-1, keepdims=True)
    centred = values - row_mean
    spread = jnp.mean(centred * centred, axis=-1, keepdims=True)
    inverse = lax.rsqrt(spread + EPS)
    return centred * inverse, inverse


def norm_back(incoming, normed, inverse):
    first = jnp.mean(incoming, axis=-1, keepdims=True)
    second = jnp.mean(incoming * normed, axis=-1, keepdims=True)
    return inverse * (incoming - first - normed * second)


def silu_slope(values):
    sig = sigmoid(values)
    return sig * (1.0 + values * (1.0 - sig))


def kernel(
    ctx_count, data_count, head_count, level_count, scale_table,
    len_ref, table_ref, stamps_hbm, x_hbm, wp_hbm, wo_hbm, go_hbm,
    layer_hbm, grad_hbm, gt_ref,
    stamps_ref, xv, wp, wo, go, normed_ref, pre_ref, gate_ref, kv_all, st_all, scol, steps,
    q_all, g_all, qs, gs, buckets, sc, wt, mix, dq, own, tab1, tab2, tacc, layer_v, grad_v,
    load_sem, out_sem, st_send, st_recv, kv_send, kv_recv, q_send, q_recv, g_send, g_recv,
    t1_send, t1_recv, t2_send, t2_recv,
):
    rows, model_dim = xv.shape
    att = wo.shape[0]
    head_dim = att // head_count
    per = LANES // head_dim
    groups = att // LANES
    score_scale = head_dim ** (-0.5)
    me = lax.axis_index("ctx")
    my_dp = lax.axis_index("dp")
    ctx_at = lambda rank: {"ctx": rank}
    dp_at = lambda rank: {"dp": rank}

    def remote(src, dst, send_sem, recv_sem, where):
        return pltpu.make_async_remote_copy(
            src_ref=src, dst_ref=dst, send_sem=send_sem, recv_sem=recv_sem,
            device_id=where, device_id_type=MESH,
        )

    def loop(low, high, body):
        def step(index, carry):
            body(index)
            return carry

        lax.fori_loop(low, high, step, 0)

    load_x = pltpu.make_async_copy(x_hbm, xv, load_sem.at[0])
    load_kv = pltpu.make_async_copy(
        wp_hbm.at[:, pl.ds(2 * att, 2 * att)], wp.at[:, pl.ds(2 * att, 2 * att)], load_sem.at[1]
    )
    load_uq = pltpu.make_async_copy(
        wp_hbm.at[:, pl.ds(0, 2 * att)], wp.at[:, pl.ds(0, 2 * att)], load_sem.at[2]
    )
    load_go = pltpu.make_async_copy(go_hbm, go, load_sem.at[3])
    load_wo = pltpu.make_async_copy(wo_hbm, wo, load_sem.at[4])
    load_st = pltpu.make_async_copy(stamps_hbm, stamps_ref, load_sem.at[5])
    for load in (load_st, load_x, load_kv, load_uq, load_go, load_wo):
        load.start()

    barrier = pltpu.get_barrier_semaphore()
    ctx_peer = lambda offset: lax.rem(me + offset, ctx_count)
    dp_peer = lambda offset: lax.rem(my_dp + offset, data_count)

    @functools.partial(loop, 1, ctx_count)
    def _(offset):
        pl.semaphore_signal(
            barrier, inc=1, device_id=ctx_at(ctx_peer(offset)), device_id_type=MESH
        )

    @functools.partial(loop, 1, data_count)
    def _(offset):
        pl.semaphore_signal(
            barrier, inc=1, device_id=dp_at(dp_peer(offset)), device_id_type=MESH
        )

    length = len_ref[0]
    for head in range(head_count):
        running = table_ref[head, 0]
        steps[0, head] = running
        for level in range(level_count - 1):
            running = running + (table_ref[head, level + 1] - table_ref[head, level])
            steps[level + 1, head] = running

    load_st.wait()
    stamp_row = stamps_ref[...]
    st_all[me] = jnp.broadcast_to(stamp_row, (8, LANES))
    scol[...] = jnp.broadcast_to(stamp_row, (rows, LANES)).T

    load_x.wait()
    normed, inverse = norm_rows(xv[...].astype(F32))
    normed_ref[...] = normed
    rounded = normed.astype(BF16)
    load_kv.wait()
    pre_kv = mul(rounded, wp[:, 2 * att :])
    pre_ref[:, 2 * att :] = pre_kv
    kv_all[me] = (pre_kv * sigmoid(pre_kv)).astype(BF16)

    pl.semaphore_wait(barrier, ctx_count - 1 + data_count - 1)

    @functools.partial(loop, 1, ctx_count)
    def _(offset):
        rank = ctx_peer(offset)
        remote(
            st_all.at[me], st_all.at[me], st_send.at[rank], st_recv.at[me], ctx_at(rank)
        ).start()

    @functools.partial(loop, me + 1, ctx_count)
    def _(rank):
        remote(
            kv_all.at[me], kv_all.at[me], kv_send.at[rank], kv_recv.at[me], ctx_at(rank)
        ).start()

    lane = lax.broadcasted_iota(jnp.int32, (rows, LANES), 1)
    part = lane // head_dim

    def stack(values, target, slot):
        for group in range(groups):
            block = values[:, group * LANES : (group + 1) * LANES]
            for index in range(per):
                target[slot, group, index * rows : (index + 1) * rows, :] = jnp.where(
                    part == index, block, 0.0
                ).astype(BF16)

    def unstack(source):
        columns = []
        for group in range(groups):
            block = source[group, :rows, :]
            for index in range(1, per):
                block = jnp.where(
                    part == index, source[group, index * rows : (index + 1) * rows, :], block
                )
            columns.append(block)
        return jnp.concatenate(columns, axis=1)

    load_uq.wait()
    pre_uq = mul(rounded, wp[:, : 2 * att])
    pre_ref[:, : 2 * att] = pre_uq
    act_uq = pre_uq * sigmoid(pre_uq)
    gate_ref[...] = act_uq[:, :att].astype(BF16).astype(F32)
    own_q = act_uq[:, att:] * score_scale
    q_all[me] = own_q.astype(BF16)

    @functools.partial(loop, 0, me)
    def _(rank):
        remote(
            q_all.at[me], q_all.at[me], q_send.at[rank], q_recv.at[me], ctx_at(rank)
        ).start()

    stack(own_q, qs, me)
    load_go.wait()
    load_wo.wait()
    grad_gated = mul(go[...], wo[...], NT)

    chunk = 32

    def add_bias(block, columns, key_stamps):
        for first in range(0, rows, chunk):
            gap = columns[first : first + chunk, :] - key_stamps
            bucket = jnp.zeros(gap.shape, jnp.int32)
            bias = [jnp.full(gap.shape, steps[0, head], F32) for head in range(head_count)]
            for level in range(level_count - 1):
                above = gap >= (1 << level)
                bucket = jnp.where(above, level + 1, bucket)
                bias = [
                    jnp.where(above, steps[level + 1, head], bias[head])
                    for head in range(head_count)
                ]
            buckets[block, first : first + chunk, :] = bucket
            for head in range(head_count):
                start = (head % per) * rows + first
                sc[block, head // per, start : start + chunk, :] = bias[head]

    def wait_stamps(rank):
        remote(
            st_all.at[rank], st_all.at[rank], st_send.at[rank], st_recv.at[rank], ctx_at(rank)
        ).wait_recv()

    @functools.partial(loop, 0, me + 1)
    def _(turn):
        block = me - turn

        @pl.when(turn > 0)
        def _():
            wait_stamps(block)

        add_bias(block, scol[...], st_all[block][0:1, :])

    def score_block(block, query_at, first_query, first_key, keys_at):
        query_pos = first_query * rows + lax.broadcasted_iota(jnp.int32, (rows, LANES), 0)
        share = 1.0 / (jnp.minimum(query_pos, length - 1) + 1).astype(F32)
        key_pos = first_key * rows + lane
        part_share = jnp.where((key_pos <= query_pos) & (key_pos < length), share, 0.0)
        shares = jnp.concatenate([part_share] * per, axis=0)
        for group in range(groups):
            keys = kv_all[keys_at, :, group * LANES : (group + 1) * LANES]
            scores = mul(qs[query_at, group], keys, NT) + sc[block, group]
            sig = sigmoid(scores)
            shared = sig * shares
            sc[block, group] = shared * (1.0 + scores * (1.0 - sig))
            wt[block, group] = (scores * shared).astype(BF16)

    mix[...] = jnp.zeros_like(mix)
    dq[...] = jnp.zeros_like(dq)

    @functools.partial(loop, 0, me + 1)
    def _(turn):
        block = me - turn

        @pl.when(turn > 0)
        def _():
            remote(
                kv_all.at[block], kv_all.at[block], kv_send.at[block], kv_recv.at[block],
                ctx_at(block),
            ).wait_recv()

        score_block(block, me, me, block, block)
        for group in range(groups):
            values = kv_all[block, :, att + group * LANES : att + (group + 1) * LANES]
            mix[group] += mul(wt[block, group], values)

    mixed_norm, mixed_inv = norm_rows(unstack(mix))
    gate = gate_ref[...]
    grad_units = grad_gated * mixed_norm
    own_g = norm_back(grad_gated * gate, mixed_norm, mixed_inv)
    g_all[me] = own_g.astype(BF16)

    @functools.partial(loop, 0, me)
    def _(rank):
        remote(
            g_all.at[me], g_all.at[me], g_send.at[rank], g_recv.at[me], ctx_at(rank)
        ).start()

    stack(own_g, gs, me)

    @functools.partial(loop, me + 1, ctx_count)
    def _(block):
        wait_stamps(block)
        stamp_block = jnp.broadcast_to(st_all[block][0:1, :], (rows, LANES))
        add_bias(block, stamp_block.T, st_all[me][0:1, :])
        remote(
            q_all.at[block], q_all.at[block], q_send.at[block], q_recv.at[block], ctx_at(block)
        ).wait_recv()
        stack(q_all[block].astype(F32), qs, block)
        score_block(block, block, block, me, me)

    def back_scores(block, query_at, keys_at, group):
        values = kv_all[keys_at, :, att + group * LANES : att + (group + 1) * LANES]
        return (mul(gs[query_at, group], values, NT) * sc[block, group]).astype(BF16)

    def add_key_grads(block, group, grad_scores):
        low, high = group * LANES, (group + 1) * LANES
        own[:, low:high] += mul(grad_scores, qs[block, group], TN)
        own[:, att + low : att + high] += mul(wt[block, group], gs[block, group], TN)

    own[...] = jnp.zeros_like(own)

    @functools.partial(loop, 0, me + 1)
    def _(block):
        for group in range(groups):
            keys = kv_all[block, :, group * LANES : (group + 1) * LANES]
            grad_scores = back_scores(block, me, block, group)
            sc[block, group] = grad_scores.astype(F32)
            dq[group] += mul(grad_scores, keys)

            @pl.when(block == me)
            def _():
                add_key_grads(block, group, grad_scores)

    tacc[...] = jnp.zeros_like(tacc)

    @functools.partial(loop, 0, me + 1)
    def _(block):
        bucket = buckets[block]
        for level in range(level_count):
            found = bucket == level
            for head in range(head_count):
                start = (head % per) * rows
                terms = jnp.where(found, sc[block, head // per, start : start + rows, :], 0.0)
                tacc[head, level] += jnp.sum(terms.reshape(rows // 8, 8, LANES), axis=0)

    cells = head_count * level_count
    summed = jnp.concatenate(
        [
            jnp.sum(tacc[...], axis=2).reshape(cells, LANES),
            jnp.zeros((LANES - cells, LANES), F32),
        ],
        axis=0,
    )
    local = jnp.broadcast_to(jnp.sum(summed.T, axis=0, keepdims=True), (8, LANES))
    tab1[me] = local

    @functools.partial(loop, 1, ctx_count)
    def _(offset):
        rank = ctx_peer(offset)
        remote(
            tab1.at[me], tab1.at[me], t1_send.at[rank], t1_recv.at[me], ctx_at(rank)
        ).start()

    gated = (mixed_norm * gate).astype(BF16)
    layer_v[...] = (xv[...].astype(F32) + mul(gated, wo[...])).astype(BF16)
    write_layer = pltpu.make_async_copy(layer_v, layer_hbm, out_sem.at[0])
    write_layer.start()

    pre_ref[:, 2 * att :] = silu_slope(pre_ref[:, 2 * att :])
    slope_uq = silu_slope(pre_ref[:, : 2 * att])
    grad_uq = jnp.concatenate([grad_units, unstack(dq) * score_scale], axis=1) * slope_uq
    grad_normed = mul(grad_uq.astype(BF16), wp[:, : 2 * att], NT)

    @functools.partial(loop, me + 1, ctx_count)
    def _(rank):
        remote(
            g_all.at[rank], g_all.at[rank], g_send.at[rank], g_recv.at[rank], ctx_at(rank)
        ).wait_recv()
        stack(g_all[rank].astype(F32), gs, rank)
        for group in range(groups):
            add_key_grads(rank, group, back_scores(rank, rank, me, group))

    @functools.partial(loop, 1, ctx_count)
    def _(offset):
        rank = ctx_peer(offset)
        remote(
            tab1.at[rank], tab1.at[rank], t1_send.at[rank], t1_recv.at[rank], ctx_at(rank)
        ).wait_recv()

    group_sum = tab1[0]
    for rank in range(1, ctx_count):
        group_sum = group_sum + tab1[rank]
    tab2[my_dp] = group_sum

    @functools.partial(loop, 1, data_count)
    def _(offset):
        rank = dp_peer(offset)
        remote(
            tab2.at[my_dp], tab2.at[my_dp], t2_send.at[rank], t2_recv.at[my_dp], dp_at(rank)
        ).start()

    grad_kv = own[...] * pre_ref[:, 2 * att :]
    grad_normed = grad_normed + mul(grad_kv.astype(BF16), wp[:, 2 * att :], NT)
    grad_v[...] = (
        norm_back(grad_normed, normed_ref[...], inverse) + go[...].astype(F32)
    ).astype(BF16)
    write_grad = pltpu.make_async_copy(grad_v, grad_hbm, out_sem.at[1])
    write_grad.start()

    @functools.partial(loop, 1, data_count)
    def _(offset):
        rank = dp_peer(offset)
        remote(
            tab2.at[rank], tab2.at[rank], t2_send.at[rank], t2_recv.at[rank], dp_at(rank)
        ).wait_recv()

    total = tab2[0]
    for rank in range(1, data_count):
        total = total + tab2[rank]
    for head in range(head_count):
        cells = total[0:1, head * level_count : (head + 1) * level_count]
        gt_ref[head : head + 1, :] = cells * scale_table

    @functools.partial(loop, me + 1, ctx_count)
    def _(rank):
        remote(
            kv_all.at[me], kv_all.at[me], kv_send.at[rank], kv_recv.at[me], ctx_at(rank)
        ).wait_send()

    @functools.partial(loop, 0, me)
    def _(block):
        remote(
            q_all.at[me], q_all.at[me], q_send.at[block], q_recv.at[me], ctx_at(block)
        ).wait_send()
        remote(
            g_all.at[me], g_all.at[me], g_send.at[block], g_recv.at[me], ctx_at(block)
        ).wait_send()

    @functools.partial(loop, 1, ctx_count)
    def _(offset):
        rank = ctx_peer(offset)
        remote(
            tab1.at[me], tab1.at[me], t1_send.at[rank], t1_recv.at[me], ctx_at(rank)
        ).wait_send()
        remote(
            st_all.at[me], st_all.at[me], st_send.at[rank], st_recv.at[me], ctx_at(rank)
        ).wait_send()

    @functools.partial(loop, 1, data_count)
    def _(offset):
        rank = dp_peer(offset)
        remote(
            tab2.at[my_dp], tab2.at[my_dp], t2_send.at[rank], t2_recv.at[my_dp], dp_at(rank)
        ).wait_send()

    write_layer.wait()
    write_grad.wait()


def hand_over(*refs):
    sources, targets, held = refs[:3], refs[3:6], refs[6:9]
    in_sems, out_sems = refs[9:]
    loads, stores = [], []
    for source, target, buffer in zip(sources, targets, held):
        size = min(64, source.shape[0])
        for first in range(0, source.shape[0], size):
            part, index = pl.ds(first, size), len(loads)
            loads.append(
                pltpu.make_async_copy(source.at[part], buffer.at[part], in_sems.at[index])
            )
            stores.append(
                pltpu.make_async_copy(buffer.at[part], target.at[part], out_sems.at[index])
            )
    for load in loads:
        load.start()
    for load, store in zip(loads, stores):
        load.wait()
        store.start()
    for store in stores:
        store.wait()


def on_device(actions, stamps, lengths, w_proj, w_out, bias_table, grad_out):
    rows = actions.shape[1]
    model_dim = actions.shape[2]
    level_count, head_count = bias_table.shape
    att = w_out.shape[0]
    ctx_count = lax.axis_size("ctx")
    data_count = lax.axis_size("dp")
    groups = att // LANES
    per = LANES // (att // head_count)
    scale_table = 1.0 / math.sqrt(rows * ctx_count * data_count)
    vmem = pl.BlockSpec(memory_space=pltpu.VMEM)
    smem = pl.BlockSpec(memory_space=pltpu.SMEM)
    anywhere = pl.BlockSpec(memory_space=pltpu.HBM)
    dma = pltpu.SemaphoreType.DMA
    layer_rows, grad_rows, grad_table = pl.pallas_call(
        functools.partial(kernel, ctx_count, data_count, head_count, level_count, scale_table),
        out_shape=(
            jax.ShapeDtypeStruct((rows, model_dim), BF16),
            jax.ShapeDtypeStruct((rows, model_dim), BF16),
            jax.ShapeDtypeStruct((head_count, level_count), F32),
        ),
        in_specs=[smem, smem, anywhere, anywhere, anywhere, anywhere, anywhere],
        out_specs=(anywhere, anywhere, vmem),
        scratch_shapes=[
            pltpu.VMEM((1, rows), jnp.int32),
            pltpu.VMEM((rows, model_dim), BF16),
            pltpu.VMEM((model_dim, 4 * att), BF16),
            pltpu.VMEM((att, model_dim), BF16),
            pltpu.VMEM((rows, model_dim), BF16),
            pltpu.VMEM((rows, model_dim), F32),
            pltpu.VMEM((rows, 4 * att), F32),
            pltpu.VMEM((rows, att), F32),
            pltpu.VMEM((ctx_count, rows, 2 * att), BF16),
            pltpu.VMEM((ctx_count, 8, LANES), jnp.int32),
            pltpu.VMEM((rows, LANES), jnp.int32),
            pltpu.SMEM((level_count, head_count), F32),
            pltpu.VMEM((ctx_count, rows, att), BF16),
            pltpu.VMEM((ctx_count, rows, att), BF16),
            pltpu.VMEM((ctx_count, groups, per * rows, LANES), BF16),
            pltpu.VMEM((ctx_count, groups, per * rows, LANES), BF16),
            pltpu.VMEM((ctx_count, rows, LANES), jnp.int32),
            pltpu.VMEM((ctx_count, groups, per * rows, LANES), F32),
            pltpu.VMEM((ctx_count, groups, per * rows, LANES), BF16),
            pltpu.VMEM((groups, per * rows, LANES), F32),
            pltpu.VMEM((groups, per * rows, LANES), F32),
            pltpu.VMEM((rows, 2 * att), F32),
            pltpu.VMEM((ctx_count, 8, LANES), F32),
            pltpu.VMEM((data_count, 8, LANES), F32),
            pltpu.VMEM((head_count, level_count, 8, LANES), F32),
            pltpu.VMEM((rows, model_dim), BF16),
            pltpu.VMEM((rows, model_dim), BF16),
            dma((6,)),
            dma((2,)),
            dma((ctx_count,)),
            dma((ctx_count,)),
            dma((ctx_count,)),
            dma((ctx_count,)),
            dma((ctx_count,)),
            dma((ctx_count,)),
            dma((ctx_count,)),
            dma((ctx_count,)),
            dma((ctx_count,)),
            dma((ctx_count,)),
            dma((data_count,)),
            dma((data_count,)),
        ],
        compiler_params=pltpu.CompilerParams(
            collective_id=0, has_side_effects=True, vmem_limit_bytes=60 * 1024 * 1024
        ),
    )(
        lengths,
        bias_table.T,
        stamps,
        actions.reshape(rows, model_dim),
        w_proj,
        w_out,
        grad_out.reshape(rows, model_dim),
    )
    results = (layer_rows, grad_rows, grad_table)
    layer_rows, grad_rows, grad_table = pl.pallas_call(
        hand_over,
        out_shape=tuple(jax.ShapeDtypeStruct(one.shape, one.dtype) for one in results),
        in_specs=[anywhere] * 3,
        out_specs=(anywhere,) * 3,
        scratch_shapes=[pltpu.VMEM(one.shape, one.dtype) for one in results]
        + [dma((2 * (rows // 64) + 1,))] * 2,
        compiler_params=pltpu.CompilerParams(vmem_limit_bytes=60 * 1024 * 1024),
    )(*results)
    return (
        layer_rows.reshape(1, rows, model_dim),
        grad_rows.reshape(1, rows, model_dim),
        grad_table.T,
    )


def solution(mesh):
    in_specs = (P("dp", "ctx", None), P("dp", "ctx"), P("dp"), P(), P(), P(), P("dp", "ctx", None))
    out_specs = (P("dp", "ctx", None), P("dp", "ctx", None), P())
    return jax.shard_map(
        on_device, mesh=mesh, in_specs=in_specs, out_specs=out_specs, check_vma=False
    )
```
